256 devices in a mesh: pa: 256 (over z, y, x, core).
Axes of the slice: x: 4, y: 4, z: 8, core: 2. Of those that a mesh axis runs over, the one named last changes fastest.
Arguments:
- coefficients: bfloat16 [196608, 3072], P('pa'), may hold values from -40 to 40, as said below
- masks: int32 [196608, 48], P('pa'), may hold values 0 or 1
Outputs:
- correlation_band: bfloat16 [196608, 3840], P('pa')
The draws below stay inside these ranges and needn't reach their ends.
Inputs may be any that keep to these rules, and one draw needn't show every extreme that they name: `coefficients`: real parts in the first 1536 columns, imaginary parts in the last 1536.
All inputs are finite; a program needn't handle non-finite values. No bound on the sum of `masks` on one device may be relied on, other than what follows from the above.
Results may differ from the reference program's by a relative error of at most 0.001.
Values may be sent and summed in bfloat16 or wider, within the bound.
A program may use at most 192 MiB of HBM per device.

```python
import jax
import jax.numpy as jnp
from jax import lax

K = 1536
G = 48
R = 768
NPART = 196608
N_PA = 256


def draw_coefficients(key, part):
    key = jax.random.fold_in(key, 7)
    class_key, shape_key, noise_key, scale_key = jax.random.split(key, 4)
    classes = jax.random.randint(class_key, (NPART,), 0, 16)
    templates = jax.random.normal(shape_key, (16, 2 * K), jnp.float32)
    signal = templates[classes]
    noise_part = jnp.clip(jax.random.normal(noise_key, (NPART, 2 * K), jnp.float32), -6.0, 6.0)
    amplitude = jnp.exp(jax.random.uniform(scale_key, (NPART, 1), jnp.float32, -0.7, 0.7))
    signal = jnp.clip(signal, -6.0, 6.0)
    return (amplitude * (signal + noise_part)).astype(jnp.bfloat16)


def place_ends(result, rng, smallest, high):
    longest = result.shape.index(max(result.shape))
    spots = []
    for shift in (0, 1):
        where = [jax.random.randint(jax.random.fold_in(rng, axis), (), 0, length) for axis, length in enumerate(result.shape)]
        where[longest] = (where[longest] + shift) % result.shape[longest]
        spots.append(tuple(where))
    return result.at[spots[0]].set(smallest).at[spots[1]].set(high)


def setup_inputs(seed: int = 0) -> dict:
    streams_of = jax.random.split(jax.random.key(seed), 3)
    return {
        "coefficients": draw_coefficients(jax.random.fold_in(streams_of[2], 71), 0),
        "masks": place_ends((jax.random.randint(streams_of[1], (NPART, G), 0, 4) < 3).astype(jnp.int32), jax.random.fold_in(streams_of[1], 1), 0, 1),
    }


ridge_term = 1.0

def prepare(coeff, mask_rows):
    rows = coeff.shape[0]
    mask_float = mask_rows.astype(jnp.float32)
    expanded = (mask_float[:, :, None] * jnp.ones((1, 1, K // G), jnp.float32)).reshape(rows, K)
    expanded = jnp.concatenate([expanded, expanded], axis=1).astype(jnp.bfloat16)
    masked = coeff * expanded
    squared = masked.astype(jnp.float32) ** 2
    power_sum = (squared[:, :K] + squared[:, K:]).reshape(rows, G, K // G).sum(axis=2)
    return (masked, mask_float, power_sum)

def score_tile(first, second):
    numerator = lax.dot_general(first[0], second[0], (((1,), (1,)), ((), ())), preferred_element_type=jnp.float32)
    norm_left = jnp.dot(first[2], second[1].T, precision=lax.Precision.HIGHEST)
    norm_right = jnp.dot(first[1], second[2].T, precision=lax.Precision.HIGHEST)
    return numerator / jnp.sqrt((norm_left + ridge_term) * (norm_right + ridge_term))

def reference(coefficients, masks):
    blocks_coeff = coefficients.reshape(N_PA, R, 2 * K)
    blocks_mask = masks.reshape(N_PA, R, G)

    def one_block(block):
        own_parts = prepare(blocks_coeff[block], blocks_mask[block])
        next_one = (block + 1) % N_PA
        next_two = (block + 2) % N_PA
        first_parts = prepare(blocks_coeff[next_one], blocks_mask[next_one])
        second_parts = prepare(blocks_coeff[next_two], blocks_mask[next_two])
        return jnp.stack([score_tile(own_parts, own_parts), score_tile(own_parts, first_parts), score_tile(own_parts, second_parts)]).astype(jnp.bfloat16)
    tiles = lax.map(one_block, jnp.arange(N_PA, dtype=jnp.int32))
    centre_tile = tiles[:, 0]
    upper_tile = tiles[:, 1]
    upper_far = tiles[:, 2]
    lower_tile = jnp.swapaxes(jnp.roll(upper_tile, 1, axis=0), 1, 2)
    lower_far = jnp.swapaxes(jnp.roll(upper_far, 2, axis=0), 1, 2)
    band = jnp.concatenate([lower_far, lower_tile, centre_tile, upper_tile, upper_far], axis=2)
    return band.reshape(N_PA * R, 5 * R)
```

```python
import functools

import jax
import jax.numpy as jnp
from jax import lax
from jax.experimental import pallas as pl
from jax.experimental.pallas import tpu as pltpu
from jax.sharding import PartitionSpec as P

K = 1536
G = 48
R = 768
BF = jnp.bfloat16
F32 = jnp.float32
MESH = pl.DeviceIdType.MESH

ridge_term = 1.0

CH = 128
NCH = R // CH
LW = 256
ROWS = 256
KP = 256


def nt(x, y):
    return lax.dot_general(x, y, (((1,), (1,)), ((), ())), preferred_element_type=F32)


def nn(x, y):
    return jnp.dot(x, y, preferred_element_type=F32)


def tn(x, y):
    return lax.dot_general(x, y, (((0,), (0,)), ((), ())), preferred_element_type=F32)


def iota(shape, dim):
    return lax.broadcasted_iota(jnp.int32, shape, dim)


def remote(src, dst, send_sem, recv_sem, device):
    return pltpu.make_async_remote_copy(
        src_ref=src, dst_ref=dst, send_sem=send_sem, recv_sem=recv_sem,
        device_id=(device,), device_id_type=MESH,
    )


def rows_of(c):
    return pl.ds(pl.multiple_of(c * CH, CH), CH)


def kernel(n, coeff, masks, out, a, s, e, pa, ma, ps, ms, pe, me, mt, mte, far, fart,
           expand, rep, mask_in, load_sem, mask_sem,
           eb_send, eb_recv, em_send, em_recv, sb_send, sb_recv, sp_send, sp_recv,
           fe_send, fe_recv, fs_send, fs_recv):
    d = lax.axis_index("pa")
    odd = lax.rem(d, 2)
    sib = d + 1 - 2 * odd
    ext = lax.rem(d + n + 2 * odd - 1, n)
    band_s = (3 - 2 * odd) * R
    band_e = (1 + 2 * odd) * R
    band_far_e = 4 * odd * R
    band_far_s = (4 - 4 * odd) * R
    band_sib_far = 4 * odd * R
    band_ext_far = (4 - 4 * odd) * R

    def cols(band, c):
        return pl.ds(pl.multiple_of(band + c * CH, CH), CH)

    def whole(band):
        return pl.ds(pl.multiple_of(band, R), R)

    load_mask = pltpu.make_async_copy(masks, mask_in, mask_sem)
    load_mask.start()

    def load(c):
        return pltpu.make_async_copy(coeff.at[rows_of(c), :], a.at[rows_of(c), :], load_sem.at[c])

    def block_to_ext(c):
        return remote(coeff.at[rows_of(c), :], e.at[rows_of(c), :], eb_send.at[c], eb_recv.at[c], ext)

    def block_to_sib(c):
        return remote(a.at[rows_of(c), :], s.at[rows_of(c), :], sb_send.at[c], sb_recv.at[c], sib)

    def far_to_ext(c):
        return remote(fart.at[rows_of(c), :], out.at[rows_of(c), whole(band_ext_far)],
                      fe_send.at[c], fe_recv.at[c], ext)

    def far_to_sib(c):
        return remote(far.at[:, cols(0, c)], out.at[:, cols(band_sib_far, c)],
                      fs_send.at[c], fs_recv.at[c], sib)

    mask_to_ext = remote(mt, mte, em_send, em_recv, ext)
    m_to_sib = remote(ma, ms, sp_send.at[0], sp_recv.at[0], sib)
    p_to_sib = remote(pa, ps, sp_send.at[1], sp_recv.at[1], sib)

    barrier = pltpu.get_barrier_semaphore()
    pl.semaphore_signal(barrier, inc=1, device_id=(sib,), device_id_type=MESH)
    pl.semaphore_signal(barrier, inc=1, device_id=(ext,), device_id_type=MESH)
    pl.loop(0, NCH)(lambda c: load(c).start())
    pl.semaphore_wait(barrier, 2)

    block_to_ext(0).start()

    load_mask.wait()
    mt[...] = mask_in[...].astype(F32).astype(BF)
    mask_to_ext.start()
    pl.loop(1, NCH)(lambda c: block_to_ext(c).start())
    rep[...] = jnp.where(
        (lax.rem(iota((G, LW), 1), G) == iota((G, LW), 0)) & (iota((G, LW), 1) < 3 * G), 1.0, 0.0
    ).astype(BF)
    ma[...] = tn(mt[...], rep[...]).astype(BF)
    m_to_sib.start()
    expand[...] = jnp.where(
        iota((LW, K), 1) // (K // G) == iota((LW, K), 0), 1.0, 0.0
    ).astype(BF)

    lane = iota((CH, LW), 1)

    def split(x):
        first = x.astype(BF)
        rest = x - first.astype(F32)
        second = rest.astype(BF)
        return first, second, (rest - second.astype(F32)).astype(BF)

    def prepare(c, block, m, p):
        rows = rows_of(c)
        m_rows = m[rows, :]
        power = jnp.zeros((CH, LW), F32)
        for k in range(0, K, KP):
            keep = nn(m_rows, expand[:, k:k + KP]).astype(BF)
            re = block[rows, k:k + KP] * keep
            im = block[rows, K + k:K + k + KP] * keep
            block[rows, k:k + KP] = re
            block[rows, K + k:K + k + KP] = im
            re = re.astype(F32)
            im = im.astype(F32)
            group = jnp.where(
                (lax.rem(iota((KP, LW), 1), G) == (iota((KP, LW), 0) + k) // (K // G))
                & (iota((KP, LW), 1) < 3 * G), 1.0, 0.0
            ).astype(BF)
            for part in split(re * re + im * im):
                power += nn(part, group)
        first, second, third = split(power)
        p[rows, :] = jnp.where(lane < G, first, jnp.where(lane < 2 * G, second, third))

    def score(x, px, mx, i, y, py, my, c):
        left = pl.ds(i, ROWS)
        right = rows_of(c)
        numerator = nt(x[left, :], y[right, :])
        norm_left = nt(px[left, :], my[right, :])
        norm_right = nt(mx[left, :], py[right, :])
        return numerator * lax.rsqrt((norm_left + ridge_term) * (norm_right + ridge_term))

    def near(c, y, py, my, band):
        for i in range(0, R, ROWS):
            out[i:i + ROWS, cols(band, c)] = score(a, pa, ma, i, y, py, my, c).astype(BF)

    @pl.loop(0, NCH)
    def _(c):
        load(c).wait()
        prepare(c, a, ma, pa)
        block_to_sib(c).start()

    p_to_sib.start()

    @pl.loop(0, NCH)
    def _(c):
        near(c, a, pa, ma, 2 * R)

    m_to_sib.wait_recv()
    p_to_sib.wait_recv()

    @pl.loop(0, NCH)
    def _(c):
        block_to_sib(c).wait_recv()
        near(c, s, ps, ms, band_s)

    mask_to_ext.wait_recv()
    me[...] = tn(mte[...], rep[...]).astype(BF)

    @pl.loop(0, NCH)
    def _(c):
        block_to_ext(c).wait_recv()
        prepare(c, e, me, pe)
        for i in range(0, R, ROWS):
            tile = score(s, ps, ms, i, e, pe, me, c)
            fart[rows_of(c), i:i + ROWS] = tile.T.astype(BF)
            far[i:i + ROWS, cols(0, c)] = tile.astype(BF)
        far_to_ext(c).start()
        far_to_sib(c).start()
        near(c, e, pe, me, band_e)

    mask_to_ext.wait_send()
    m_to_sib.wait_send()
    p_to_sib.wait_send()

    @pl.loop(0, NCH)
    def _(c):
        block_to_ext(c).wait_send()
        block_to_sib(c).wait_send()
        far_to_sib(c).wait()
        far_to_ext(c).wait()


def on_device(coefficients, masks):
    n = lax.axis_size("pa")
    block = pltpu.VMEM((R, 2 * K), BF)
    norm = pltpu.VMEM((R, LW), BF)
    dma = pltpu.SemaphoreType.DMA
    return pl.pallas_call(
        functools.partial(kernel, n),
        out_shape=pltpu.VMEM((R, 5 * R), BF),
        in_specs=[pl.BlockSpec(memory_space=pltpu.HBM)] * 2,
        out_specs=pl.BlockSpec(memory_space=pltpu.VMEM),
        scratch_shapes=[
            block, block, block, norm, norm, norm, norm, norm, norm,
            pltpu.VMEM((G, R), BF), pltpu.VMEM((G, R), BF),
            pltpu.VMEM((R, R), BF), pltpu.VMEM((R, R), BF),
            pltpu.VMEM((LW, K), BF), pltpu.VMEM((G, LW), BF),
            pltpu.VMEM((G, R), jnp.int32),
            dma((NCH,)), dma,
            dma((NCH,)), dma((NCH,)), dma, dma, dma((NCH,)), dma((NCH,)), dma((2,)), dma((2,)),
            dma((NCH,)), dma((NCH,)), dma((NCH,)), dma((NCH,)),
        ],
        compiler_params=pltpu.CompilerParams(
            collective_id=0, has_side_effects=True, vmem_limit_bytes=56 * 1024 * 1024
        ),
        cost_estimate=pl.CostEstimate(
            flops=2 * 4 * R * R * 2 * K, bytes_accessed=4 * R * 2 * K, transcendentals=4 * R * R
        ),
        name="band",
    )(coefficients, masks.T)


def solution(mesh):
    return jax.shard_map(
        on_device, mesh=mesh, in_specs=(P("pa", None), P("pa", None)),
        out_specs=P("pa", None), check_vma=False,
    )
```

```python
import functools

import jax
import jax.numpy as jnp
from jax import lax
from jax.experimental import pallas as pl
from jax.experimental.pallas import tpu as pltpu
from jax.sharding import PartitionSpec as P

K = 1536
G = 48
R = 768
BF = jnp.bfloat16
F32 = jnp.float32
MESH = pl.DeviceIdType.MESH

ridge_term = 1.0

CH = 128
NCH = R // CH
LW = 256
ROWS = 256
KP = 256


def nt(x, y):
    return lax.dot_general(x, y, (((1,), (1,)), ((), ())), preferred_element_type=F32)


def nn(x, y):
    return jnp.dot(x, y, preferred_element_type=F32)


def tn(x, y):
    return lax.dot_general(x, y, (((0,), (0,)), ((), ())), preferred_element_type=F32)


def iota(shape, dim):
    return lax.broadcasted_iota(jnp.int32, shape, dim)


def remote(src, dst, send_sem, recv_sem, device):
    return pltpu.make_async_remote_copy(
        src_ref=src, dst_ref=dst, send_sem=send_sem, recv_sem=recv_sem,
        device_id=(device,), device_id_type=MESH,
    )


def rows_of(c):
    return pl.ds(pl.multiple_of(c * CH, CH), CH)


def kernel(n, coeff, masks, out, a, s, e, pa, ma, ps, ms, pe, me, mt, mte, far, fart,
           expand, rep, mask_in, load_sem, mask_sem,
           eb_send, eb_recv, em_send, em_recv, sb_send, sb_recv, sp_send, sp_recv,
           fe_send, fe_recv, fs_send, fs_recv):
    d = lax.axis_index("pa")
    odd = lax.rem(d, 2)
    sib = d + 1 - 2 * odd
    ext = lax.rem(d + n + 2 * odd - 1, n)
    band_s = (3 - 2 * odd) * R
    band_e = (1 + 2 * odd) * R
    band_far_e = 4 * odd * R
    band_far_s = (4 - 4 * odd) * R
    band_sib_far = 4 * odd * R
    band_ext_far = (4 - 4 * odd) * R

    def cols(band, c):
        return pl.ds(pl.multiple_of(band + c * CH, CH), CH)

    def whole(band):
        return pl.ds(pl.multiple_of(band, R), R)

    load_mask = pltpu.make_async_copy(masks, mask_in, mask_sem)
    load_mask.start()

    def load(c):
        return pltpu.make_async_copy(coeff.at[rows_of(c), :], a.at[rows_of(c), :], load_sem.at[c])

    def block_to_ext(c):
        return remote(coeff.at[rows_of(c), :], e.at[rows_of(c), :], eb_send.at[c], eb_recv.at[c], ext)

    def block_to_sib(c):
        return remote(a.at[rows_of(c), :], s.at[rows_of(c), :], sb_send.at[c], sb_recv.at[c], sib)

    def far_to_ext(c):
        return remote(fart.at[rows_of(c), :], out.at[rows_of(c), whole(band_ext_far)],
                      fe_send.at[c], fe_recv.at[c], ext)

    def far_to_sib(c):
        return remote(far.at[:, cols(0, c)], out.at[:, cols(band_sib_far, c)],
                      fs_send.at[c], fs_recv.at[c], sib)

    mask_to_ext = remote(mt, mte, em_send, em_recv, ext)
    m_to_sib = remote(ma, ms, sp_send.at[0], sp_recv.at[0], sib)
    p_to_sib = remote(pa, ps, sp_send.at[1], sp_recv.at[1], sib)

    barrier = pltpu.get_barrier_semaphore()
    pl.semaphore_signal(barrier, inc=1, device_id=(sib,), device_id_type=MESH)
    pl.semaphore_signal(barrier, inc=1, device_id=(ext,), device_id_type=MESH)
    pl.loop(0, NCH)(lambda c: load(c).start())
    pl.semaphore_wait(barrier, 2)

    block_to_ext(0).start()

    load_mask.wait()
    mt[...] = mask_in[...].astype(F32).astype(BF)
    mask_to_ext.start()
    pl.loop(1, NCH)(lambda c: block_to_ext(c).start())
    rep[...] = jnp.where(
        (lax.rem(iota((G, LW), 1), G) == iota((G, LW), 0)) & (iota((G, LW), 1) < 3 * G), 1.0, 0.0
    ).astype(BF)
    ma[...] = tn(mt[...], rep[...]).astype(BF)
    m_to_sib.start()
    expand[...] = jnp.where(
        iota((LW, K), 1) // (K // G) == iota((LW, K), 0), 1.0, 0.0
    ).astype(BF)

    lane = iota((CH, LW), 1)

    def split(x):
        first = x.astype(BF)
        rest = x - first.astype(F32)
        second = rest.astype(BF)
        return first, second, (rest - second.astype(F32)).astype(BF)

    def prepare(c, block, m, p):
        rows = rows_of(c)
        m_rows = m[rows, :]
        power = jnp.zeros((CH, LW), F32)
        for k in range(0, K, KP):
            keep = nn(m_rows, expand[:, k:k + KP]).astype(BF)
            re = block[rows, k:k + KP] * keep
            im = block[rows, K + k:K + k + KP] * keep
            block[rows, k:k + KP] = re
            block[rows, K + k:K + k + KP] = im
            re = re.astype(F32)
            im = im.astype(F32)
            group = jnp.where(
                (lax.rem(iota((KP, LW), 1), G) == (iota((KP, LW), 0) + k) // (K // G))
                & (iota((KP, LW), 1) < 3 * G), 1.0, 0.0
            ).astype(BF)
            for part in split(re * re + im * im):
                power += nn(part, group)
        first, second, third = split(power)
        p[rows, :] = jnp.where(lane < G, first, jnp.where(lane < 2 * G, second, third))

    def score(x, px, mx, i, y, py, my, c):
        left = pl.ds(i, ROWS)
        right = rows_of(c)
        numerator = nt(x[left, :], y[right, :])
        norm_left = nt(px[left, :], my[right, :])
        norm_right = nt(mx[left, :], py[right, :])
        return numerator * lax.rsqrt((norm_left + ridge_term) * (norm_right + ridge_term))

    def near(c, y, py, my, band):
        for i in range(0, R, ROWS):
            out[i:i + ROWS, cols(band, c)] = score(a, pa, ma, i, y, py, my, c).astype(BF)

    @pl.loop(0, NCH)
    def _(c):
        load(c).wait()
        prepare(c, a, ma, pa)
        block_to_sib(c).start()

    p_to_sib.start()

    @pl.loop(0, NCH)
    def _(c):
        near(c, a, pa, ma, 2 * R)

    m_to_sib.wait_recv()
    p_to_sib.wait_recv()

    @pl.loop(0, NCH)
    def _(c):
        block_to_sib(c).wait_recv()
        near(c, s, ps, ms, band_s)

    mask_to_ext.wait_recv()
    me[...] = tn(mte[...], rep[...]).astype(BF)

    def far_tile(c):
        prepare(c, e, me, pe)
        for i in range(0, R, ROWS):
            tile = score(s, ps, ms, i, e, pe, me, c)
            fart[rows_of(c), i:i + ROWS] = tile.T.astype(BF)
            far[i:i + ROWS, cols(0, c)] = tile.astype(BF)

    @pl.loop(0, NCH)
    def _(c):
        @pl.when(c == NCH - 1)
        def _():
            far_to_ext(0).start()
            block_to_ext(NCH - 1).wait_send()
            pl.loop(1, NCH - 1)(lambda j: far_to_ext(j).start())

        block_to_ext(c).wait_recv()
        far_tile(c)

        @pl.when(c == NCH - 1)
        def _():
            far_to_ext(c).start()

        far_to_sib(c).start()
        near(c, e, pe, me, band_e)

    mask_to_ext.wait_send()
    m_to_sib.wait_send()
    p_to_sib.wait_send()
    pl.loop(0, NCH - 1)(lambda c: block_to_ext(c).wait_send())

    @pl.loop(0, NCH)
    def _(c):
        block_to_sib(c).wait_send()
        far_to_sib(c).wait()
        far_to_ext(c).wait()


def on_device(coefficients, masks):
    n = lax.axis_size("pa")
    block = pltpu.VMEM((R, 2 * K), BF)
    norm = pltpu.VMEM((R, LW), BF)
    dma = pltpu.SemaphoreType.DMA
    return pl.pallas_call(
        functools.partial(kernel, n),
        out_shape=pltpu.VMEM((R, 5 * R), BF),
        in_specs=[pl.BlockSpec(memory_space=pltpu.HBM)] * 2,
        out_specs=pl.BlockSpec(memory_space=pltpu.VMEM),
        scratch_shapes=[
            block, block, block, norm, norm, norm, norm, norm, norm,
            pltpu.VMEM((G, R), BF), pltpu.VMEM((G, R), BF),
            pltpu.VMEM((R, R), BF), pltpu.VMEM((R, R), BF),
            pltpu.VMEM((LW, K), BF), pltpu.VMEM((G, LW), BF),
            pltpu.VMEM((G, R), jnp.int32),
            dma((NCH,)), dma,
            dma((NCH,)), dma((NCH,)), dma, dma, dma((NCH,)), dma((NCH,)), dma((2,)), dma((2,)),
            dma((NCH,)), dma((NCH,)), dma((NCH,)), dma((NCH,)),
        ],
        compiler_params=pltpu.CompilerParams(
            collective_id=0, has_side_effects=True, vmem_limit_bytes=56 * 1024 * 1024
        ),
        cost_estimate=pl.CostEstimate(
            flops=2 * 4 * R * R * 2 * K, bytes_accessed=4 * R * 2 * K, transcendentals=4 * R * R
        ),
        name="band",
    )(coefficients, masks.T)


def solution(mesh):
    return jax.shard_map(
        on_device, mesh=mesh, in_specs=(P("pa", None), P("pa", None)),
        out_specs=P("pa", None), check_vma=False,
    )
```

```python
import functools

import jax
import jax.numpy as jnp
from jax import lax
from jax.experimental import pallas as pl
from jax.experimental.pallas import tpu as pltpu
from jax.sharding import PartitionSpec as P

K = 1536
G = 48
R = 768
BF = jnp.bfloat16
F32 = jnp.float32
MESH = pl.DeviceIdType.MESH

ridge_term = 1.0

CH = 256
NCH = R // CH
LATE = CH // 2
NSEND = NCH + 1
LW = 256
ROWS = 768
KP = 256

NX = 4
NY = 4
RR = 32


def nt(x, y):
    return lax.dot_general(x, y, (((1,), (1,)), ((), ())), preferred_element_type=F32)


def nn(x, y):
    return jnp.dot(x, y, preferred_element_type=F32)


def tn(x, y):
    return lax.dot_general(x, y, (((0,), (0,)), ((), ())), preferred_element_type=F32)


def iota(shape, dim):
    return lax.broadcasted_iota(jnp.int32, shape, dim)


def lane_group(shape):
    lane = iota(shape, 1)
    lane = jnp.where(lane < G, lane, jnp.where(lane < 2 * G, lane - G, lane - 2 * G))
    return jnp.where(iota(shape, 1) < 3 * G, lane, K)


def remote(src, dst, send_sem, recv_sem, device):
    return pltpu.make_async_remote_copy(
        src_ref=src, dst_ref=dst, send_sem=send_sem, recv_sem=recv_sem,
        device_id=(device,), device_id_type=MESH,
    )


def rows_of(c):
    return pl.ds(pl.multiple_of(c * CH, CH), CH)


def late_rows(c):
    return pl.ds(pl.multiple_of(R - CH + c * LATE, LATE), LATE)


def kernel(n, coeff, masks, out, a, s, e, pa, ma, ps, ms, pe, me, mt, mte, far, fart,
           expand, group, rep, mask_in, load_sem, mask_sem,
           rb, to_send, to_recv, on_send, on_recv, leave, eb_send, eb_recv, em_send, em_recv, sb_send, sb_recv, sp_send, sp_recv,
           fe_send, fe_recv, fs_send, fs_recv):
    d = lax.axis_index("pa")
    odd = lax.rem(d, 2)
    sib = d + 1 - 2 * odd
    ext = lax.rem(d + n + 2 * odd - 1, n)
    band_s = (3 - 2 * odd) * R
    band_e = (1 + 2 * odd) * R
    band_far_e = 4 * odd * R
    band_far_s = (4 - 4 * odd) * R
    band_sib_far = 4 * odd * R
    band_ext_far = (4 - 4 * odd) * R

    row = 2 * NX
    plane = row * NY
    place = lax.rem(d, plane)
    base = d - place
    below = lax.rem(base + n - plane, n)
    above = lax.rem(base + plane, n)
    is_last = place == plane - 1
    is_first = place == 0
    is_end = is_last | is_first
    is_up = place == row - 2
    is_down = place == plane - row + 1
    is_relay = is_up | is_down
    relay_out = base + jnp.where(is_last, row - 2, plane - row + 1)
    relay_in = jnp.where(is_last, above + plane - row + 1, below + row - 2)
    relay_from = base + jnp.where(is_up, plane - 1, 0)
    relay_to = jnp.where(is_up, above, below + plane - 1)

    def cols(band, rows):
        return pl.ds(pl.multiple_of(band + rows.start, rows.size), rows.size)

    def whole(band):
        return pl.ds(pl.multiple_of(band, R), R)

    load_mask = pltpu.make_async_copy(masks, mask_in, mask_sem)
    load_mask.start()

    def load(c):
        return pltpu.make_async_copy(coeff.at[rows_of(c), :], a.at[rows_of(c), :], load_sem.at[c])

    def to_ext(rows, c):
        return remote(coeff.at[rows, :], e.at[rows, :], eb_send.at[c], eb_recv.at[c], ext)

    def block_to_ext(c):
        return to_ext(rows_of(c), c)

    late_to_ext = to_ext(late_rows(0), NCH - 1)
    most_to_ext = to_ext(pl.ds(R - LATE, LATE - RR), NCH)
    rest = pl.ds(R - RR, RR)
    rest_to_ext = to_ext(rest, NCH + 1)
    to_relay = remote(coeff.at[rest, :], rb, to_send, to_recv, relay_out)
    from_relay = remote(rb, e.at[rest, :], on_send, on_recv, relay_to)

    def block_to_sib(c):
        return remote(a.at[rows_of(c), :], s.at[rows_of(c), :], sb_send.at[c], sb_recv.at[c], sib)

    def far_to_ext(rows, c):
        return remote(fart.at[rows, :], out.at[rows, whole(band_ext_far)],
                      fe_send.at[c], fe_recv.at[c], ext)

    def far_to_sib(rows, c):
        return remote(far.at[:, cols(0, rows)], out.at[:, cols(band_sib_far, rows)],
                      fs_send.at[c], fs_recv.at[c], sib)

    mask_to_ext = remote(mt, mte, em_send, em_recv, ext)
    m_to_sib = remote(ma, ms, sp_send.at[0], sp_recv.at[0], sib)
    p_to_sib = remote(pa, ps, sp_send.at[1], sp_recv.at[1], sib)

    barrier = pltpu.get_barrier_semaphore()
    pl.semaphore_signal(barrier, inc=1, device_id=(sib,), device_id_type=MESH)
    pl.semaphore_signal(barrier, inc=1, device_id=(ext,), device_id_type=MESH)

    @pl.when(is_relay)
    def _():
        pl.semaphore_signal(barrier, inc=1, device_id=(relay_from,), device_id_type=MESH)
        pl.semaphore_signal(barrier, inc=1, device_id=(relay_to,), device_id_type=MESH)

    pl.loop(0, NCH)(lambda c: load(c).start())
    pl.semaphore_wait(barrier, jnp.where(is_end, 4, 2))

    block_to_ext(0).start()

    @pl.when(is_end)
    def _():
        to_relay.start()
        pl.semaphore_signal(leave, inc=1, device_id=(relay_in,), device_id_type=MESH)


    load_mask.wait()
    mt[...] = mask_in[...].astype(F32).astype(BF)
    mask_to_ext.start()
    pl.loop(1, NCH - 1)(lambda c: block_to_ext(c).start())
    late_to_ext.start()
    most_to_ext.start()

    @pl.when(jnp.logical_not(is_end))
    def _():
        rest_to_ext.start()

    rep[...] = jnp.where(lane_group((G, LW)) == iota((G, LW), 0), 1.0, 0.0).astype(BF)
    ma[...] = tn(mt[...], rep[...]).astype(BF)
    m_to_sib.start()
    for k in range(0, K, KP):
        first = iota((LW, KP), 0) * (K // G)
        column = iota((LW, KP), 1) + k
        expand[:, k:k + KP] = jnp.where(
            (column >= first) & (column < first + K // G), 1.0, 0.0
        ).astype(BF)
        first = lane_group((KP, LW)) * (K // G)
        column = iota((KP, LW), 0) + k
        group[k:k + KP, :] = jnp.where(
            (column >= first) & (column < first + K // G), 1.0, 0.0
        ).astype(BF)

    def split(x):
        first = x.astype(BF)
        rest = x - first.astype(F32)
        second = rest.astype(BF)
        return first, second, (rest - second.astype(F32)).astype(BF)

    def prepare(rows, block, m, p):
        count = rows.size
        m_rows = m[rows, :]
        power = jnp.zeros((count, LW), F32)
        for k in range(0, K, KP):
            keep = nn(m_rows, expand[:, k:k + KP]).astype(BF)
            re = block[rows, k:k + KP] * keep
            im = block[rows, K + k:K + k + KP] * keep
            block[rows, k:k + KP] = re
            block[rows, K + k:K + k + KP] = im
            re = re.astype(F32)
            im = im.astype(F32)
            parts = nn(jnp.concatenate(split(re * re + im * im), axis=0), group[k:k + KP, :])
            power += parts[:count] + parts[count:2 * count] + parts[2 * count:]
        first, second, third = split(power)
        lane = iota((count, LW), 1)
        p[rows, :] = jnp.where(lane < G, first, jnp.where(lane < 2 * G, second, third))

    def score(x, px, mx, left, y, py, my, right):
        numerator = nt(x[left, :], y[right, :])
        norm_left = nt(px[left, :], my[right, :])
        norm_right = nt(mx[left, :], py[right, :])
        return numerator * lax.rsqrt((norm_left + ridge_term) * (norm_right + ridge_term))

    def near(rows, y, py, my, band):
        for i in range(0, R, ROWS):
            left = pl.ds(i, ROWS)
            out[left, cols(band, rows)] = score(a, pa, ma, left, y, py, my, rows).astype(BF)

    @pl.loop(0, NCH)
    def _(c):
        load(c).wait()
        prepare(rows_of(c), a, ma, pa)
        block_to_sib(c).start()

    p_to_sib.start()

    @pl.when(is_relay)
    def _():
        pl.semaphore_wait(leave, 1)
        to_relay.wait_recv()
        from_relay.start()

    @pl.loop(0, NCH)
    def _(c):
        near(rows_of(c), a, pa, ma, 2 * R)

    m_to_sib.wait_recv()
    p_to_sib.wait_recv()

    @pl.loop(0, NCH)
    def _(c):
        block_to_sib(c).wait_recv()
        near(rows_of(c), s, ps, ms, band_s)

    mask_to_ext.wait_recv()
    me[...] = tn(mte[...], rep[...]).astype(BF)

    def with_ext(rows, c):
        prepare(rows, e, me, pe)
        for i in range(0, R, ROWS):
            left = pl.ds(i, ROWS)
            tile = score(s, ps, ms, left, e, pe, me, rows)
            fart[rows, left] = tile.T.astype(BF)
            far[left, cols(0, rows)] = tile.astype(BF)
        far_to_ext(rows, c).start()
        far_to_sib(rows, c).start()
        near(rows, e, pe, me, band_e)

    @pl.loop(0, NCH - 1)
    def _(c):
        block_to_ext(c).wait_recv()
        with_ext(rows_of(c), c)

    @pl.loop(0, 2)
    def _(c):
        @pl.when(c == 0)
        def _():
            late_to_ext.wait_recv()

        @pl.when(c == 1)
        def _():
            most_to_ext.wait_recv()
            pl.when(is_end)(from_relay.wait_recv)
            pl.when(jnp.logical_not(is_end))(rest_to_ext.wait_recv)

        with_ext(late_rows(c), NCH - 1 + c)

    mask_to_ext.wait_send()
    m_to_sib.wait_send()
    p_to_sib.wait_send()
    late_to_ext.wait_send()
    most_to_ext.wait_send()
    pl.when(is_end)(to_relay.wait_send)
    pl.when(jnp.logical_not(is_end))(rest_to_ext.wait_send)
    pl.when(is_relay)(from_relay.wait_send)
    pl.loop(0, NCH - 1)(lambda c: block_to_ext(c).wait_send())
    pl.loop(0, NCH)(lambda c: block_to_sib(c).wait_send())

    @pl.loop(0, NCH - 1)
    def _(c):
        far_to_sib(rows_of(c), c).wait()
        far_to_ext(rows_of(c), c).wait()

    @pl.loop(0, 2)
    def _(c):
        far_to_sib(late_rows(c), NCH - 1 + c).wait()
        far_to_ext(late_rows(c), NCH - 1 + c).wait()


def on_device(coefficients, masks):
    n = lax.axis_size("pa")
    block = pltpu.VMEM((R, 2 * K), BF)
    norm = pltpu.VMEM((R, LW), BF)
    dma = pltpu.SemaphoreType.DMA
    return pl.pallas_call(
        functools.partial(kernel, n),
        out_shape=pltpu.VMEM((R, 5 * R), BF),
        in_specs=[pl.BlockSpec(memory_space=pltpu.HBM)] * 2,
        out_specs=pl.BlockSpec(memory_space=pltpu.VMEM),
        scratch_shapes=[
            block, block, block, norm, norm, norm, norm, norm, norm,
            pltpu.VMEM((G, R), BF), pltpu.VMEM((G, R), BF),
            pltpu.VMEM((R, R), BF), pltpu.VMEM((R, R), BF),
            pltpu.VMEM((LW, K), BF), pltpu.VMEM((K, LW), BF), pltpu.VMEM((G, LW), BF),
            pltpu.VMEM((G, R), jnp.int32),
            dma((NCH,)), dma,
            pltpu.VMEM((RR, 2 * K), BF), dma, dma, dma, dma, pltpu.SemaphoreType.REGULAR,
            dma((NCH + 2,)), dma((NCH + 2,)), dma, dma,
            dma((NCH,)), dma((NCH,)), dma((2,)), dma((2,)),
            dma((NSEND,)), dma((NSEND,)), dma((NSEND,)), dma((NSEND,)),
        ],
        compiler_params=pltpu.CompilerParams(
            collective_id=0, has_side_effects=True, vmem_limit_bytes=56 * 1024 * 1024
        ),
        cost_estimate=pl.CostEstimate(
            flops=2 * 4 * R * R * 2 * K, bytes_accessed=4 * R * 2 * K, transcendentals=4 * R * R
        ),
        name="band",
    )(coefficients, masks.T)


def solution(mesh):
    return jax.shard_map(
        on_device, mesh=mesh, in_specs=(P("pa", None), P("pa", None)),
        out_specs=P("pa", None), check_vma=False,
    )
```

```python
import functools

import jax
import jax.numpy as jnp
from jax import lax
from jax.experimental import pallas as pl
from jax.experimental.pallas import tpu as pltpu
from jax.sharding import PartitionSpec as P

K = 1536
G = 48
R = 768
BF = jnp.bfloat16
F32 = jnp.float32
MESH = pl.DeviceIdType.MESH

ridge_term = 1.0

CH = 256
NCH = R // CH
LATE = CH // 2
NSEND = NCH + 1
LW = 256
ROWS = 768
KP = 256

NX = 4
NY = 4
RR = 48


def nt(x, y):
    return lax.dot_general(x, y, (((1,), (1,)), ((), ())), preferred_element_type=F32)


def nn(x, y):
    return jnp.dot(x, y, preferred_element_type=F32)


def tn(x, y):
    return lax.dot_general(x, y, (((0,), (0,)), ((), ())), preferred_element_type=F32)


def iota(shape, dim):
    return lax.broadcasted_iota(jnp.int32, shape, dim)


def lane_group(shape):
    lane = iota(shape, 1)
    lane = jnp.where(lane < G, lane, jnp.where(lane < 2 * G, lane - G, lane - 2 * G))
    return jnp.where(iota(shape, 1) < 3 * G, lane, K)


def remote(src, dst, send_sem, recv_sem, device):
    return pltpu.make_async_remote_copy(
        src_ref=src, dst_ref=dst, send_sem=send_sem, recv_sem=recv_sem,
        device_id=(device,), device_id_type=MESH,
    )


def rows_of(c):
    return pl.ds(pl.multiple_of(c * CH, CH), CH)


def late_rows(c):
    return pl.ds(pl.multiple_of(R - CH + c * LATE, LATE), LATE)


def kernel(n, coeff, masks, out, a, s, e, pa, ma, ps, ms, pe, me, mt, mte, far, fart,
           expand, group, rep, mask_in, load_sem, mask_sem,
           rb, hub_send, hub_recv, spoke_send, spoke_recv, on_send, on_recv, leave, eb_send, eb_recv, em_send, em_recv, sb_send, sb_recv, sp_send, sp_recv,
           fe_send, fe_recv, fs_send, fs_recv):
    d = lax.axis_index("pa")
    odd = lax.rem(d, 2)
    sib = d + 1 - 2 * odd
    ext = lax.rem(d + n + 2 * odd - 1, n)
    band_s = (3 - 2 * odd) * R
    band_e = (1 + 2 * odd) * R
    band_far_e = 4 * odd * R
    band_far_s = (4 - 4 * odd) * R
    band_sib_far = 4 * odd * R
    band_ext_far = (4 - 4 * odd) * R

    row = 2 * NX
    plane = row * NY
    place = lax.rem(d, plane)
    base = d - place
    below = lax.rem(base + n - plane, n)
    above = lax.rem(base + plane, n)
    is_last = place == plane - 1
    is_first = place == 0
    is_end = is_last | is_first
    level = place // row
    is_up = (lax.rem(place, row) == row - 2) & (level < 2)
    is_down = (lax.rem(place, row) == 1) & (level >= NY - 2)
    level = jnp.where(is_up, level, NY - 1 - level)
    is_hub = (is_up | is_down) & (level == 0)
    is_spoke = (is_up | is_down) & (level == 1)
    step = jnp.where(is_up, row, -row)
    hub_from = base + jnp.where(is_up, plane - 1, 0)
    relay_to = jnp.where(is_up, above, below + plane - 1)
    hub_out = base + jnp.where(is_last, row - 2, plane - row + 1)
    hub_in = jnp.where(is_last, above + plane - row + 1, below + row - 2)
    spoke_in = hub_in + jnp.where(is_last, -row, row)

    def cols(band, rows):
        return pl.ds(pl.multiple_of(band + rows.start, rows.size), rows.size)

    def whole(band):
        return pl.ds(pl.multiple_of(band, R), R)

    load_mask = pltpu.make_async_copy(masks, mask_in, mask_sem)
    load_mask.start()

    def load(c):
        return pltpu.make_async_copy(coeff.at[rows_of(c), :], a.at[rows_of(c), :], load_sem.at[c])

    def to_ext(rows, c):
        return remote(coeff.at[rows, :], e.at[rows, :], eb_send.at[c], eb_recv.at[c], ext)

    def block_to_ext(c):
        return to_ext(rows_of(c), c)

    late_to_ext = to_ext(late_rows(0), NCH - 1)
    most_to_ext = to_ext(pl.ds(R - LATE, LATE - RR), NCH)
    rest = pl.ds(R - RR, RR)
    rest_to_ext = to_ext(rest, NCH + 1)
    reals, imags = pl.ds(0, K), pl.ds(K, K)
    to_hub = remote(coeff.at[rest, :], rb, hub_send, hub_recv, hub_out)
    to_spoke = remote(rb.at[:, imags], rb.at[:, imags], spoke_send, spoke_recv, d + step)
    from_hub = remote(rb.at[:, reals], e.at[rest, reals], on_send, on_recv.at[0], relay_to)
    from_spoke = remote(rb.at[:, imags], e.at[rest, imags], on_send, on_recv.at[1], relay_to)

    def block_to_sib(c):
        return remote(a.at[rows_of(c), :], s.at[rows_of(c), :], sb_send.at[c], sb_recv.at[c], sib)

    def far_to_ext(rows, c):
        return remote(fart.at[rows, :], out.at[rows, whole(band_ext_far)],
                      fe_send.at[c], fe_recv.at[c], ext)

    def far_to_sib(rows, c):
        return remote(far.at[:, cols(0, rows)], out.at[:, cols(band_sib_far, rows)],
                      fs_send.at[c], fs_recv.at[c], sib)

    mask_to_ext = remote(mt, mte, em_send, em_recv, ext)
    m_to_sib = remote(ma, ms, sp_send.at[0], sp_recv.at[0], sib)
    p_to_sib = remote(pa, ps, sp_send.at[1], sp_recv.at[1], sib)

    barrier = pltpu.get_barrier_semaphore()
    pl.semaphore_signal(barrier, inc=1, device_id=(sib,), device_id_type=MESH)
    pl.semaphore_signal(barrier, inc=1, device_id=(ext,), device_id_type=MESH)

    def greet(device):
        pl.semaphore_signal(barrier, inc=1, device_id=(device,), device_id_type=MESH)

    @pl.when(is_hub)
    def _():
        greet(hub_from)
        greet(relay_to)

    @pl.when(is_spoke)
    def _():
        greet(d - step)
        greet(relay_to)

    pl.loop(0, NCH)(lambda c: load(c).start())
    pl.semaphore_wait(barrier, jnp.where(is_end, 5, jnp.where(is_hub, 3, 2)))

    block_to_ext(0).start()

    @pl.when(is_end)
    def _():
        to_hub.start()
        for relay in (hub_in, spoke_in):
            pl.semaphore_signal(leave, inc=1, device_id=(relay,), device_id_type=MESH)

    load_mask.wait()
    mt[...] = mask_in[...].astype(F32).astype(BF)
    mask_to_ext.start()
    pl.loop(1, NCH - 1)(lambda c: block_to_ext(c).start())
    late_to_ext.start()
    most_to_ext.start()
    pl.when(jnp.logical_not(is_end))(rest_to_ext.start)

    rep[...] = jnp.where(lane_group((G, LW)) == iota((G, LW), 0), 1.0, 0.0).astype(BF)
    ma[...] = tn(mt[...], rep[...]).astype(BF)
    m_to_sib.start()
    for k in range(0, K, KP):
        first = iota((LW, KP), 0) * (K // G)
        column = iota((LW, KP), 1) + k
        expand[:, k:k + KP] = jnp.where(
            (column >= first) & (column < first + K // G), 1.0, 0.0
        ).astype(BF)
        first = lane_group((KP, LW)) * (K // G)
        column = iota((KP, LW), 0) + k
        group[k:k + KP, :] = jnp.where(
            (column >= first) & (column < first + K // G), 1.0, 0.0
        ).astype(BF)

    def split(x):
        first = x.astype(BF)
        rest = x - first.astype(F32)
        second = rest.astype(BF)
        return first, second, (rest - second.astype(F32)).astype(BF)

    def prepare(rows, block, m, p):
        count = rows.size
        m_rows = m[rows, :]
        power = jnp.zeros((count, LW), F32)
        for k in range(0, K, KP):
            keep = nn(m_rows, expand[:, k:k + KP]).astype(BF)
            re = block[rows, k:k + KP] * keep
            im = block[rows, K + k:K + k + KP] * keep
            block[rows, k:k + KP] = re
            block[rows, K + k:K + k + KP] = im
            re = re.astype(F32)
            im = im.astype(F32)
            parts = nn(jnp.concatenate(split(re * re + im * im), axis=0), group[k:k + KP, :])
            power += parts[:count] + parts[count:2 * count] + parts[2 * count:]
        first, second, third = split(power)
        lane = iota((count, LW), 1)
        p[rows, :] = jnp.where(lane < G, first, jnp.where(lane < 2 * G, second, third))

    def score(x, px, mx, left, y, py, my, right):
        numerator = nt(x[left, :], y[right, :])
        norm_left = nt(px[left, :], my[right, :])
        norm_right = nt(mx[left, :], py[right, :])
        return numerator * lax.rsqrt((norm_left + ridge_term) * (norm_right + ridge_term))

    def near(rows, y, py, my, band):
        for i in range(0, R, ROWS):
            left = pl.ds(i, ROWS)
            out[left, cols(band, rows)] = score(a, pa, ma, left, y, py, my, rows).astype(BF)

    @pl.loop(0, NCH)
    def _(c):
        load(c).wait()
        prepare(rows_of(c), a, ma, pa)
        block_to_sib(c).start()

    p_to_sib.start()

    @pl.when(is_hub)
    def _():
        to_hub.wait_recv()
        to_spoke.start()
        pl.semaphore_wait(leave, 1)
        from_hub.start()

    @pl.loop(0, NCH)
    def _(c):
        near(rows_of(c), a, pa, ma, 2 * R)

    m_to_sib.wait_recv()
    p_to_sib.wait_recv()

    @pl.loop(0, NCH)
    def _(c):
        block_to_sib(c).wait_recv()
        near(rows_of(c), s, ps, ms, band_s)

    @pl.when(is_spoke)
    def _():
        to_spoke.wait_recv()
        pl.semaphore_wait(leave, 1)
        from_spoke.start()

    mask_to_ext.wait_recv()
    me[...] = tn(mte[...], rep[...]).astype(BF)

    def with_ext(rows, c):
        prepare(rows, e, me, pe)
        tile = score(e, pe, me, rows, s, ps, ms, pl.ds(0, R))
        fart[rows, :] = tile.astype(BF)
        far_to_ext(rows, c).start()
        far[:, cols(0, rows)] = tile.T.astype(BF)
        far_to_sib(rows, c).start()
        near(rows, e, pe, me, band_e)

    @pl.loop(0, NCH - 1)
    def _(c):
        block_to_ext(c).wait_recv()
        with_ext(rows_of(c), c)

    @pl.loop(0, 2)
    def _(c):
        @pl.when(c == 0)
        def _():
            late_to_ext.wait_recv()

        @pl.when(c == 1)
        def _():
            most_to_ext.wait_recv()
            pl.when(jnp.logical_not(is_end))(rest_to_ext.wait_recv)

            @pl.when(is_end)
            def _():
                from_hub.wait_recv()
                from_spoke.wait_recv()

        with_ext(late_rows(c), NCH - 1 + c)

    mask_to_ext.wait_send()
    m_to_sib.wait_send()
    p_to_sib.wait_send()
    late_to_ext.wait_send()
    most_to_ext.wait_send()
    pl.when(is_end)(to_hub.wait_send)
    pl.when(jnp.logical_not(is_end))(rest_to_ext.wait_send)
    pl.when(is_spoke)(from_spoke.wait_send)

    @pl.when(is_hub)
    def _():
        to_spoke.wait_send()
        from_hub.wait_send()

    pl.loop(0, NCH - 1)(lambda c: block_to_ext(c).wait_send())
    pl.loop(0, NCH)(lambda c: block_to_sib(c).wait_send())

    @pl.loop(0, NCH - 1)
    def _(c):
        far_to_sib(rows_of(c), c).wait()
        far_to_ext(rows_of(c), c).wait()

    @pl.loop(0, 2)
    def _(c):
        far_to_sib(late_rows(c), NCH - 1 + c).wait()
        far_to_ext(late_rows(c), NCH - 1 + c).wait()


def on_device(coefficients, masks):
    n = lax.axis_size("pa")
    block = pltpu.VMEM((R, 2 * K), BF)
    norm = pltpu.VMEM((R, LW), BF)
    dma = pltpu.SemaphoreType.DMA
    return pl.pallas_call(
        functools.partial(kernel, n),
        out_shape=pltpu.VMEM((R, 5 * R), BF),
        in_specs=[pl.BlockSpec(memory_space=pltpu.HBM)] * 2,
        out_specs=pl.BlockSpec(memory_space=pltpu.VMEM),
        scratch_shapes=[
            block, block, block, norm, norm, norm, norm, norm, norm,
            pltpu.VMEM((G, R), BF), pltpu.VMEM((G, R), BF),
            pltpu.VMEM((R, R), BF), pltpu.VMEM((R, R), BF),
            pltpu.VMEM((LW, K), BF), pltpu.VMEM((K, LW), BF), pltpu.VMEM((G, LW), BF),
            pltpu.VMEM((G, R), jnp.int32),
            dma((NCH,)), dma,
            pltpu.VMEM((RR, 2 * K), BF),
            dma, dma, dma, dma, dma, dma((2,)), pltpu.SemaphoreType.REGULAR,
            dma((NCH + 2,)), dma((NCH + 2,)), dma, dma,
            dma((NCH,)), dma((NCH,)), dma((2,)), dma((2,)),
            dma((NSEND,)), dma((NSEND,)), dma((NSEND,)), dma((NSEND,)),
        ],
        compiler_params=pltpu.CompilerParams(
            collective_id=0, has_side_effects=True, vmem_limit_bytes=56 * 1024 * 1024
        ),
        cost_estimate=pl.CostEstimate(
            flops=2 * 4 * R * R * 2 * K, bytes_accessed=4 * R * 2 * K, transcendentals=4 * R * R
        ),
        name="band",
    )(coefficients, masks.T)


def solution(mesh):
    return jax.shard_map(
        on_device, mesh=mesh, in_specs=(P("pa", None), P("pa", None)),
        out_specs=P("pa", None), check_vma=False,
    )
```

```python
import functools

import jax
import jax.numpy as jnp
from jax import lax
from jax.experimental import pallas as pl
from jax.experimental.pallas import tpu as pltpu
from jax.sharding import PartitionSpec as P

K = 1536
G = 48
R = 768
BF = jnp.bfloat16
F32 = jnp.float32
MESH = pl.DeviceIdType.MESH

ridge_term = 1.0

CH = 256
NCH = R // CH
LATE = CH // 2
NSEND = NCH + 1
LW = 256
ROWS = 768
KP = 256

NX = 4
NY = 4
RR = 48
TR = 32
TC = 2304


def nt(x, y):
    return lax.dot_general(x, y, (((1,), (1,)), ((), ())), preferred_element_type=F32)


def nn(x, y):
    return jnp.dot(x, y, preferred_element_type=F32)


def tn(x, y):
    return lax.dot_general(x, y, (((0,), (0,)), ((), ())), preferred_element_type=F32)


def iota(shape, dim):
    return lax.broadcasted_iota(jnp.int32, shape, dim)


def lane_group(shape):
    lane = iota(shape, 1)
    lane = jnp.where(lane < G, lane, jnp.where(lane < 2 * G, lane - G, lane - 2 * G))
    return jnp.where(iota(shape, 1) < 3 * G, lane, K)


def remote(src, dst, send_sem, recv_sem, device):
    return pltpu.make_async_remote_copy(
        src_ref=src, dst_ref=dst, send_sem=send_sem, recv_sem=recv_sem,
        device_id=(device,), device_id_type=MESH,
    )


def rows_of(c):
    return pl.ds(pl.multiple_of(c * CH, CH), CH)


def late_rows(c):
    return pl.ds(pl.multiple_of(R - CH + c * LATE, LATE), LATE)


def kernel(n, coeff, masks, out, a, s, e, pa, ma, ps, ms, pe, me, mt, mte, far, fart,
           expand, group, rep, mask_in, load_sem, mask_sem,
           rb, turn_send, turn_recv, hub_send, hub_recv, spoke_send, spoke_recv,
           on_send, on_recv, leave, eb_send, eb_recv, em_send, em_recv, sb_send, sb_recv, sp_send, sp_recv,
           fe_send, fe_recv, fs_send, fs_recv):
    d = lax.axis_index("pa")
    odd = lax.rem(d, 2)
    sib = d + 1 - 2 * odd
    ext = lax.rem(d + n + 2 * odd - 1, n)
    band_s = (3 - 2 * odd) * R
    band_e = (1 + 2 * odd) * R
    band_far_e = 4 * odd * R
    band_far_s = (4 - 4 * odd) * R
    band_sib_far = 4 * odd * R
    band_ext_far = (4 - 4 * odd) * R

    row = 2 * NX
    plane = row * NY
    place = lax.rem(d, plane)
    base = d - place
    below = lax.rem(base + n - plane, n)
    above = lax.rem(base + plane, n)
    is_last = place == plane - 1
    is_first = place == 0
    is_end = is_last | is_first
    level = place // row
    is_up = (lax.rem(place, row) == row - 2) & (level < 2)
    is_down = (lax.rem(place, row) == 1) & (level >= NY - 2)
    column = lax.rem(place, row)
    is_edge = (column == 0) | (column == row - 1)
    is_turn_up = column == 3
    is_turn_down = column == row - 4
    is_turn = is_turn_up | is_turn_down
    row_up = base + lax.rem(level + 1, NY) * row
    row_down = base + lax.rem(level + NY - 1, NY) * row
    turn_from = jnp.where(is_turn_up, row_down + row - 1, row_up)
    turn_to = lax.rem(turn_from + n + jnp.where(is_turn_up, 1, -1), n)

    def turn_of(edge):
        at = lax.rem(edge, plane)
        level = at // row
        up = lax.rem(level + 1, NY) * row + 3
        down = lax.rem(level + NY - 1, NY) * row + row - 4
        return edge - at + jnp.where(lax.rem(edge, 2) == 1, up, down)

    turn_out = turn_of(d)
    turn_in = turn_of(ext)
    level = jnp.where(is_up, level, NY - 1 - level)
    is_hub = (is_up | is_down) & (level == 0)
    is_spoke = (is_up | is_down) & (level == 1)
    step = jnp.where(is_up, row, -row)
    hub_from = base + jnp.where(is_up, plane - 1, 0)
    relay_to = jnp.where(is_up, above, below + plane - 1)
    hub_out = base + jnp.where(is_last, row - 2, plane - row + 1)
    hub_in = jnp.where(is_last, above + plane - row + 1, below + row - 2)
    spoke_in = hub_in + jnp.where(is_last, -row, row)

    def cols(band, rows):
        return pl.ds(pl.multiple_of(band + rows.start, rows.size), rows.size)

    def whole(band):
        return pl.ds(pl.multiple_of(band, R), R)

    load_mask = pltpu.make_async_copy(masks, mask_in, mask_sem)
    load_mask.start()

    def load(c):
        return pltpu.make_async_copy(coeff.at[rows_of(c), :], a.at[rows_of(c), :], load_sem.at[c])

    def to_ext(rows, c):
        return remote(coeff.at[rows, :], e.at[rows, :], eb_send.at[c], eb_recv.at[c], ext)

    def block_to_ext(c):
        return to_ext(rows_of(c), c)

    late_to_ext = to_ext(late_rows(0), NCH - 1)
    turned = pl.ds(R - LATE, TR)
    turned_columns, kept_columns = pl.ds(0, TC), pl.ds(TC, 2 * K - TC)

    def turned_rows_to_ext(columns, c):
        return remote(coeff.at[turned, columns], e.at[turned, columns],
                      eb_send.at[c], eb_recv.at[c], ext)

    turned_to_ext = turned_rows_to_ext(turned_columns, NCH + 2)
    kept_to_ext = turned_rows_to_ext(kept_columns, NCH + 3)
    most_to_ext = to_ext(pl.ds(R - LATE + TR, LATE - TR - RR), NCH)
    at_turn = rb.at[0:TR, turned_columns]
    to_turn = remote(coeff.at[turned, turned_columns], at_turn, turn_send, turn_recv, turn_out)
    from_turn = remote(at_turn, e.at[turned, turned_columns], on_send, on_recv.at[2], turn_to)
    rest = pl.ds(R - RR, RR)
    rest_to_ext = to_ext(rest, NCH + 1)
    reals, imags = pl.ds(0, K), pl.ds(K, K)
    to_hub = remote(coeff.at[rest, :], rb, hub_send, hub_recv, hub_out)
    to_spoke = remote(rb.at[:, imags], rb.at[:, imags], spoke_send, spoke_recv, d + step)
    from_hub = remote(rb.at[:, reals], e.at[rest, reals], on_send, on_recv.at[0], relay_to)
    from_spoke = remote(rb.at[:, imags], e.at[rest, imags], on_send, on_recv.at[1], relay_to)

    def block_to_sib(c):
        return remote(a.at[rows_of(c), :], s.at[rows_of(c), :], sb_send.at[c], sb_recv.at[c], sib)

    def far_to_ext(rows, c):
        return remote(fart.at[rows, :], out.at[rows, whole(band_ext_far)],
                      fe_send.at[c], fe_recv.at[c], ext)

    def far_to_sib(rows, c):
        return remote(far.at[:, cols(0, rows)], out.at[:, cols(band_sib_far, rows)],
                      fs_send.at[c], fs_recv.at[c], sib)

    mask_to_ext = remote(mt, mte, em_send, em_recv, ext)
    m_to_sib = remote(ma, ms, sp_send.at[0], sp_recv.at[0], sib)
    p_to_sib = remote(pa, ps, sp_send.at[1], sp_recv.at[1], sib)

    barrier = pltpu.get_barrier_semaphore()
    pl.semaphore_signal(barrier, inc=1, device_id=(sib,), device_id_type=MESH)
    pl.semaphore_signal(barrier, inc=1, device_id=(ext,), device_id_type=MESH)

    def greet(device):
        pl.semaphore_signal(barrier, inc=1, device_id=(device,), device_id_type=MESH)

    @pl.when(is_hub)
    def _():
        greet(hub_from)
        greet(relay_to)

    @pl.when(is_spoke)
    def _():
        greet(d - step)
        greet(relay_to)

    @pl.when(is_turn)
    def _():
        greet(turn_from)
        greet(turn_to)

    pl.loop(0, NCH)(lambda c: load(c).start())
    greeted = jnp.where(is_end, 5, jnp.where(is_hub, 3, 2)) + jnp.where(is_edge, 2, 0)
    pl.semaphore_wait(barrier, greeted)

    block_to_ext(0).start()

    def allow(device):
        pl.semaphore_signal(leave, inc=1, device_id=(device,), device_id_type=MESH)

    @pl.when(is_edge)
    def _():
        to_turn.start()
        allow(turn_in)

    @pl.when(is_end)
    def _():
        to_hub.start()
        allow(hub_in)
        allow(spoke_in)

    load_mask.wait()
    mt[...] = mask_in[...].astype(F32).astype(BF)
    mask_to_ext.start()
    pl.loop(1, NCH - 1)(lambda c: block_to_ext(c).start())
    late_to_ext.start()
    pl.when(jnp.logical_not(is_edge))(turned_to_ext.start)
    kept_to_ext.start()
    most_to_ext.start()
    pl.when(jnp.logical_not(is_end))(rest_to_ext.start)

    rep[...] = jnp.where(lane_group((G, LW)) == iota((G, LW), 0), 1.0, 0.0).astype(BF)
    ma[...] = tn(mt[...], rep[...]).astype(BF)
    m_to_sib.start()
    for k in range(0, K, KP):
        first = iota((LW, KP), 0) * (K // G)
        column = iota((LW, KP), 1) + k
        expand[:, k:k + KP] = jnp.where(
            (column >= first) & (column < first + K // G), 1.0, 0.0
        ).astype(BF)
        first = lane_group((KP, LW)) * (K // G)
        column = iota((KP, LW), 0) + k
        group[k:k + KP, :] = jnp.where(
            (column >= first) & (column < first + K // G), 1.0, 0.0
        ).astype(BF)

    def split(x):
        first = x.astype(BF)
        rest = x - first.astype(F32)
        second = rest.astype(BF)
        return first, second, (rest - second.astype(F32)).astype(BF)

    def prepare(rows, block, m, p):
        count = rows.size
        m_rows = m[rows, :]
        power = jnp.zeros((count, LW), F32)
        for k in range(0, K, KP):
            keep = nn(m_rows, expand[:, k:k + KP]).astype(BF)
            re = block[rows, k:k + KP] * keep
            im = block[rows, K + k:K + k + KP] * keep
            block[rows, k:k + KP] = re
            block[rows, K + k:K + k + KP] = im
            re = re.astype(F32)
            im = im.astype(F32)
            parts = nn(jnp.concatenate(split(re * re + im * im), axis=0), group[k:k + KP, :])
            power += parts[:count] + parts[count:2 * count] + parts[2 * count:]
        first, second, third = split(power)
        lane = iota((count, LW), 1)
        p[rows, :] = jnp.where(lane < G, first, jnp.where(lane < 2 * G, second, third))

    def score(x, px, mx, left, y, py, my, right):
        numerator = nt(x[left, :], y[right, :])
        norm_left = nt(px[left, :], my[right, :])
        norm_right = nt(mx[left, :], py[right, :])
        return numerator * lax.rsqrt((norm_left + ridge_term) * (norm_right + ridge_term))

    def near(rows, y, py, my, band):
        for i in range(0, R, ROWS):
            left = pl.ds(i, ROWS)
            out[left, cols(band, rows)] = score(a, pa, ma, left, y, py, my, rows).astype(BF)

    @pl.loop(0, NCH)
    def _(c):
        load(c).wait()
        prepare(rows_of(c), a, ma, pa)
        block_to_sib(c).start()

    p_to_sib.start()

    @pl.when(is_turn)
    def _():
        to_turn.wait_recv()
        pl.semaphore_wait(leave, 1)
        from_turn.start()

    @pl.when(is_hub)
    def _():
        to_hub.wait_recv()
        to_spoke.start()
        pl.semaphore_wait(leave, 1)
        from_hub.start()

    @pl.loop(0, NCH)
    def _(c):
        near(rows_of(c), a, pa, ma, 2 * R)

    m_to_sib.wait_recv()
    p_to_sib.wait_recv()

    @pl.loop(0, NCH)
    def _(c):
        block_to_sib(c).wait_recv()
        near(rows_of(c), s, ps, ms, band_s)

    @pl.when(is_spoke)
    def _():
        to_spoke.wait_recv()
        pl.semaphore_wait(leave, 1)
        from_spoke.start()

    mask_to_ext.wait_recv()
    me[...] = tn(mte[...], rep[...]).astype(BF)

    def with_ext(rows, c):
        prepare(rows, e, me, pe)
        tile = score(e, pe, me, rows, s, ps, ms, pl.ds(0, R))
        fart[rows, :] = tile.astype(BF)
        far_to_ext(rows, c).start()
        far[:, cols(0, rows)] = tile.T.astype(BF)
        far_to_sib(rows, c).start()
        near(rows, e, pe, me, band_e)

    @pl.loop(0, NCH - 1)
    def _(c):
        block_to_ext(c).wait_recv()
        with_ext(rows_of(c), c)

    @pl.loop(0, 2)
    def _(c):
        @pl.when(c == 0)
        def _():
            late_to_ext.wait_recv()

        @pl.when(c == 1)
        def _():
            most_to_ext.wait_recv()
            kept_to_ext.wait_recv()
            pl.when(is_edge)(from_turn.wait_recv)
            pl.when(jnp.logical_not(is_edge))(turned_to_ext.wait_recv)
            pl.when(jnp.logical_not(is_end))(rest_to_ext.wait_recv)

            @pl.when(is_end)
            def _():
                from_hub.wait_recv()
                from_spoke.wait_recv()

        with_ext(late_rows(c), NCH - 1 + c)

    mask_to_ext.wait_send()
    m_to_sib.wait_send()
    p_to_sib.wait_send()
    late_to_ext.wait_send()
    most_to_ext.wait_send()
    kept_to_ext.wait_send()
    pl.when(is_edge)(to_turn.wait_send)
    pl.when(jnp.logical_not(is_edge))(turned_to_ext.wait_send)
    pl.when(is_turn)(from_turn.wait_send)
    pl.when(is_end)(to_hub.wait_send)
    pl.when(jnp.logical_not(is_end))(rest_to_ext.wait_send)
    pl.when(is_spoke)(from_spoke.wait_send)

    @pl.when(is_hub)
    def _():
        to_spoke.wait_send()
        from_hub.wait_send()

    pl.loop(0, NCH - 1)(lambda c: block_to_ext(c).wait_send())
    pl.loop(0, NCH)(lambda c: block_to_sib(c).wait_send())

    @pl.loop(0, NCH - 1)
    def _(c):
        far_to_sib(rows_of(c), c).wait()
        far_to_ext(rows_of(c), c).wait()

    @pl.loop(0, 2)
    def _(c):
        far_to_sib(late_rows(c), NCH - 1 + c).wait()
        far_to_ext(late_rows(c), NCH - 1 + c).wait()


def on_device(coefficients, masks):
    n = lax.axis_size("pa")
    block = pltpu.VMEM((R, 2 * K), BF)
    norm = pltpu.VMEM((R, LW), BF)
    dma = pltpu.SemaphoreType.DMA
    return pl.pallas_call(
        functools.partial(kernel, n),
        out_shape=pltpu.VMEM((R, 5 * R), BF),
        in_specs=[pl.BlockSpec(memory_space=pltpu.HBM)] * 2,
        out_specs=pl.BlockSpec(memory_space=pltpu.VMEM),
        scratch_shapes=[
            block, block, block, norm, norm, norm, norm, norm, norm,
            pltpu.VMEM((G, R), BF), pltpu.VMEM((G, R), BF),
            pltpu.VMEM((R, R), BF), pltpu.VMEM((R, R), BF),
            pltpu.VMEM((LW, K), BF), pltpu.VMEM((K, LW), BF), pltpu.VMEM((G, LW), BF),
            pltpu.VMEM((G, R), jnp.int32),
            dma((NCH,)), dma,
            pltpu.VMEM((RR, 2 * K), BF),
            dma, dma, dma, dma, dma, dma, dma, dma((3,)), pltpu.SemaphoreType.REGULAR,
            dma((NCH + 4,)), dma((NCH + 4,)), dma, dma,
            dma((NCH,)), dma((NCH,)), dma((2,)), dma((2,)),
            dma((NSEND,)), dma((NSEND,)), dma((NSEND,)), dma((NSEND,)),
        ],
        compiler_params=pltpu.CompilerParams(
            collective_id=0, has_side_effects=True, vmem_limit_bytes=56 * 1024 * 1024
        ),
        cost_estimate=pl.CostEstimate(
            flops=2 * 4 * R * R * 2 * K, bytes_accessed=4 * R * 2 * K, transcendentals=4 * R * R
        ),
        name="band",
    )(coefficients, masks.T)


def solution(mesh):
    return jax.shard_map(
        on_device, mesh=mesh, in_specs=(P("pa", None), P("pa", None)),
        out_specs=P("pa", None), check_vma=False,
    )
```

```python
import functools

import jax
import jax.numpy as jnp
from jax import lax
from jax.experimental import pallas as pl
from jax.experimental.pallas import tpu as pltpu
from jax.sharding import PartitionSpec as P

K = 1536
G = 48
R = 768
BF = jnp.bfloat16
F32 = jnp.float32
MESH = pl.DeviceIdType.MESH

ridge_term = 1.0

CH = 256
NCH = R // CH
LATE = CH // 2
NSEND = NCH + 1
LW = 256
ROWS = 768
KP = 256

NX = 4
NY = 4
RR = 48
TR = 32
TC = 2048


def nt(x, y):
    return lax.dot_general(x, y, (((1,), (1,)), ((), ())), preferred_element_type=F32)


def nn(x, y):
    return jnp.dot(x, y, preferred_element_type=F32)


def tn(x, y):
    return lax.dot_general(x, y, (((0,), (0,)), ((), ())), preferred_element_type=F32)


def iota(shape, dim):
    return lax.broadcasted_iota(jnp.int32, shape, dim)


def lane_group(shape):
    lane = iota(shape, 1)
    lane = jnp.where(lane < G, lane, jnp.where(lane < 2 * G, lane - G, lane - 2 * G))
    return jnp.where(iota(shape, 1) < 3 * G, lane, K)


def remote(src, dst, send_sem, recv_sem, device):
    return pltpu.make_async_remote_copy(
        src_ref=src, dst_ref=dst, send_sem=send_sem, recv_sem=recv_sem,
        device_id=(device,), device_id_type=MESH,
    )


def rows_of(c):
    return pl.ds(pl.multiple_of(c * CH, CH), CH)


def late_rows(c):
    return pl.ds(pl.multiple_of(R - CH + c * LATE, LATE), LATE)


def kernel(n, coeff, masks, out, a, s, e, pa, ma, ps, ms, pe, me, mt, mte, far, fart,
           expand, group, rep, mask_in, load_sem, mask_sem,
           rb, turn_send, turn_recv, hub_send, hub_recv, spoke_send, spoke_recv,
           on_send, on_recv, leave, vouch, eb_send, eb_recv, em_send, em_recv, sb_send, sb_recv, sp_send, sp_recv,
           fe_send, fe_recv, fs_send, fs_recv):
    d = lax.axis_index("pa")
    odd = lax.rem(d, 2)
    sib = d + 1 - 2 * odd
    ext = lax.rem(d + n + 2 * odd - 1, n)
    band_s = (3 - 2 * odd) * R
    band_e = (1 + 2 * odd) * R
    band_far_e = 4 * odd * R
    band_far_s = (4 - 4 * odd) * R
    band_sib_far = 4 * odd * R
    band_ext_far = (4 - 4 * odd) * R

    row = 2 * NX
    plane = row * NY
    place = lax.rem(d, plane)
    base = d - place
    below = lax.rem(base + n - plane, n)
    above = lax.rem(base + plane, n)
    is_last = place == plane - 1
    is_first = place == 0
    is_end = is_last | is_first
    level = place // row
    is_up = (lax.rem(place, row) == row - 2) & (level < 2)
    is_down = (lax.rem(place, row) == 1) & (level >= NY - 2)
    column = lax.rem(place, row)
    is_edge = (column == 0) | (column == row - 1)
    is_turn_up = column == 3
    is_turn_down = column == row - 4
    is_turn = is_turn_up | is_turn_down
    row_up = base + lax.rem(level + 1, NY) * row
    row_down = base + lax.rem(level + NY - 1, NY) * row
    turn_from = jnp.where(is_turn_up, row_down + row - 1, row_up)
    turn_to = lax.rem(turn_from + n + jnp.where(is_turn_up, 1, -1), n)

    def turn_of(edge):
        at = lax.rem(edge, plane)
        level = at // row
        up = lax.rem(level + 1, NY) * row + 3
        down = lax.rem(level + NY - 1, NY) * row + row - 4
        return edge - at + jnp.where(lax.rem(edge, 2) == 1, up, down)

    turn_out = turn_of(d)
    turn_in = turn_of(ext)
    level = jnp.where(is_up, level, NY - 1 - level)
    is_hub = (is_up | is_down) & (level == 0)
    is_spoke = (is_up | is_down) & (level == 1)
    step = jnp.where(is_up, row, -row)
    hub_from = base + jnp.where(is_up, plane - 1, 0)
    relay_to = jnp.where(is_up, above, below + plane - 1)
    hub_out = base + jnp.where(is_last, row - 2, plane - row + 1)
    hub_in = jnp.where(is_last, above + plane - row + 1, below + row - 2)
    spoke_in = hub_in + jnp.where(is_last, -row, row)

    def cols(band, rows):
        return pl.ds(pl.multiple_of(band + rows.start, rows.size), rows.size)

    def whole(band):
        return pl.ds(pl.multiple_of(band, R), R)

    load_mask = pltpu.make_async_copy(masks, mask_in, mask_sem)
    load_mask.start()

    def load(c):
        return pltpu.make_async_copy(coeff.at[rows_of(c), :], a.at[rows_of(c), :], load_sem.at[c])

    def to_ext(rows, c):
        return remote(coeff.at[rows, :], e.at[rows, :], eb_send.at[c], eb_recv.at[c], ext)

    def block_to_ext(c):
        return to_ext(rows_of(c), c)

    late_to_ext = to_ext(late_rows(0), NCH - 1)
    turned = pl.ds(R - LATE, TR)
    turned_columns, kept_columns = pl.ds(0, TC), pl.ds(TC, 2 * K - TC)

    def turned_rows_to_ext(columns, c):
        return remote(coeff.at[turned, columns], e.at[turned, columns],
                      eb_send.at[c], eb_recv.at[c], ext)

    turned_to_ext = turned_rows_to_ext(turned_columns, NCH + 2)
    kept_to_ext = turned_rows_to_ext(kept_columns, NCH + 3)
    most_to_ext = to_ext(pl.ds(R - LATE + TR, LATE - TR - RR), NCH)
    at_turn = rb.at[0:TR, turned_columns]
    to_turn = remote(coeff.at[turned, turned_columns], at_turn, turn_send, turn_recv, turn_out)
    from_turn = remote(at_turn, e.at[turned, turned_columns], on_send, on_recv.at[2], turn_to)
    rest = pl.ds(R - RR, RR)
    rest_to_ext = to_ext(rest, NCH + 1)
    reals, imags = pl.ds(0, K), pl.ds(K, K)
    to_hub = remote(coeff.at[rest, :], rb, hub_send, hub_recv, hub_out)
    to_spoke = remote(rb.at[:, imags], rb.at[:, imags], spoke_send, spoke_recv, d + step)
    from_hub = remote(rb.at[:, reals], e.at[rest, reals], on_send, on_recv.at[0], relay_to)
    from_spoke = remote(rb.at[:, imags], e.at[rest, imags], on_send, on_recv.at[1], relay_to)

    def block_to_sib(c):
        return remote(a.at[rows_of(c), :], s.at[rows_of(c), :], sb_send.at[c], sb_recv.at[c], sib)

    def far_to_ext(rows, c):
        return remote(fart.at[rows, :], out.at[rows, whole(band_ext_far)],
                      fe_send.at[c], fe_recv.at[c], ext)

    def far_to_sib(rows, c):
        return remote(far.at[:, cols(0, rows)], out.at[:, cols(band_sib_far, rows)],
                      fs_send.at[c], fs_recv.at[c], sib)

    mask_to_ext = remote(mt, mte, em_send, em_recv, ext)
    m_to_sib = remote(ma, ms, sp_send.at[0], sp_recv.at[0], sib)
    p_to_sib = remote(pa, ps, sp_send.at[1], sp_recv.at[1], sib)

    barrier = pltpu.get_barrier_semaphore()
    pl.semaphore_signal(barrier, inc=1, device_id=(sib,), device_id_type=MESH)
    pl.semaphore_signal(barrier, inc=1, device_id=(ext,), device_id_type=MESH)

    def greet(device):
        pl.semaphore_signal(barrier, inc=1, device_id=(device,), device_id_type=MESH)

    @pl.when(is_hub)
    def _():
        greet(hub_from)

    @pl.when(is_hub | is_spoke)
    def _():
        greet(relay_to)

    @pl.when(is_turn)
    def _():
        greet(turn_to)

    pl.loop(0, NCH)(lambda c: load(c).start())
    pl.semaphore_wait(barrier, jnp.where(is_end, 6, jnp.where(is_edge, 3, 2)))

    block_to_ext(0).start()

    def allow(device):
        pl.semaphore_signal(leave, inc=1, device_id=(device,), device_id_type=MESH)

    @pl.when(is_edge)
    def _():
        allow(turn_in)
        pl.semaphore_signal(vouch, inc=1, device_id=(ext,), device_id_type=MESH)

    @pl.when(is_end)
    def _():
        to_hub.start()
        allow(hub_in)
        allow(spoke_in)

    load_mask.wait()
    mt[...] = mask_in[...].astype(F32).astype(BF)
    mask_to_ext.start()
    pl.loop(1, NCH - 1)(lambda c: block_to_ext(c).start())
    late_to_ext.start()
    pl.when(jnp.logical_not(is_edge))(turned_to_ext.start)
    kept_to_ext.start()
    most_to_ext.start()
    pl.when(jnp.logical_not(is_end))(rest_to_ext.start)

    rep[...] = jnp.where(lane_group((G, LW)) == iota((G, LW), 0), 1.0, 0.0).astype(BF)
    ma[...] = tn(mt[...], rep[...]).astype(BF)
    m_to_sib.start()
    for k in range(0, K, KP):
        first = iota((LW, KP), 0) * (K // G)
        column = iota((LW, KP), 1) + k
        expand[:, k:k + KP] = jnp.where(
            (column >= first) & (column < first + K // G), 1.0, 0.0
        ).astype(BF)
        first = lane_group((KP, LW)) * (K // G)
        column = iota((KP, LW), 0) + k
        group[k:k + KP, :] = jnp.where(
            (column >= first) & (column < first + K // G), 1.0, 0.0
        ).astype(BF)

    def split(x):
        first = x.astype(BF)
        rest = x - first.astype(F32)
        second = rest.astype(BF)
        return first, second, (rest - second.astype(F32)).astype(BF)

    def prepare(rows, block, m, p):
        count = rows.size
        m_rows = m[rows, :]
        power = jnp.zeros((count, LW), F32)
        for k in range(0, K, KP):
            keep = nn(m_rows, expand[:, k:k + KP]).astype(BF)
            re = block[rows, k:k + KP] * keep
            im = block[rows, K + k:K + k + KP] * keep
            block[rows, k:k + KP] = re
            block[rows, K + k:K + k + KP] = im
            re = re.astype(F32)
            im = im.astype(F32)
            parts = nn(jnp.concatenate(split(re * re + im * im), axis=0), group[k:k + KP, :])
            power += parts[:count] + parts[count:2 * count] + parts[2 * count:]
        first, second, third = split(power)
        lane = iota((count, LW), 1)
        p[rows, :] = jnp.where(lane < G, first, jnp.where(lane < 2 * G, second, third))

    def score(x, px, mx, left, y, py, my, right):
        numerator = nt(x[left, :], y[right, :])
        norm_left = nt(px[left, :], my[right, :])
        norm_right = nt(mx[left, :], py[right, :])
        return numerator * lax.rsqrt((norm_left + ridge_term) * (norm_right + ridge_term))

    def near(rows, y, py, my, band):
        for i in range(0, R, ROWS):
            left = pl.ds(i, ROWS)
            out[left, cols(band, rows)] = score(a, pa, ma, left, y, py, my, rows).astype(BF)

    @pl.when(is_edge)
    def _():
        pl.semaphore_wait(vouch, 1)
        to_turn.start()

    @pl.loop(0, NCH)
    def _(c):
        load(c).wait()
        prepare(rows_of(c), a, ma, pa)
        block_to_sib(c).start()

    p_to_sib.start()

    @pl.when(is_turn)
    def _():
        to_turn.wait_recv()
        pl.semaphore_wait(leave, 1)
        from_turn.start()

    @pl.when(is_hub)
    def _():
        to_hub.wait_recv()
        pl.semaphore_wait(leave, 1)
        to_spoke.start()
        from_hub.start()

    @pl.loop(0, NCH)
    def _(c):
        near(rows_of(c), a, pa, ma, 2 * R)

    m_to_sib.wait_recv()
    p_to_sib.wait_recv()

    @pl.loop(0, NCH)
    def _(c):
        block_to_sib(c).wait_recv()
        near(rows_of(c), s, ps, ms, band_s)

    @pl.when(is_spoke)
    def _():
        to_spoke.wait_recv()
        pl.semaphore_wait(leave, 1)
        from_spoke.start()

    mask_to_ext.wait_recv()
    me[...] = tn(mte[...], rep[...]).astype(BF)

    def with_ext(rows, c):
        prepare(rows, e, me, pe)
        tile = score(e, pe, me, rows, s, ps, ms, pl.ds(0, R))
        fart[rows, :] = tile.astype(BF)

        @pl.when(c == NCH)
        def _():
            far_to_ext(rows, c).start()

        far[:, cols(0, rows)] = tile.T.astype(BF)
        far_to_sib(rows, c).start()
        near(rows, e, pe, me, band_e)

    @pl.loop(0, NCH - 1)
    def _(c):
        block_to_ext(c).wait_recv()
        pl.when(c > 0)(lambda: far_to_ext(rows_of(c - 1), c - 1).start())
        with_ext(rows_of(c), c)

    @pl.loop(0, 2)
    def _(c):
        @pl.when(c == 0)
        def _():
            late_to_ext.wait_recv()
            far_to_ext(rows_of(NCH - 2), NCH - 2).start()

        @pl.when(c == 1)
        def _():
            most_to_ext.wait_recv()
            kept_to_ext.wait_recv()
            pl.when(is_edge)(from_turn.wait_recv)
            pl.when(jnp.logical_not(is_edge))(turned_to_ext.wait_recv)
            pl.when(jnp.logical_not(is_end))(rest_to_ext.wait_recv)

            @pl.when(is_end)
            def _():
                from_hub.wait_recv()
                from_spoke.wait_recv()

            far_to_ext(late_rows(0), NCH - 1).start()

        with_ext(late_rows(c), NCH - 1 + c)

    mask_to_ext.wait_send()
    m_to_sib.wait_send()
    p_to_sib.wait_send()
    late_to_ext.wait_send()
    most_to_ext.wait_send()
    kept_to_ext.wait_send()
    pl.when(is_edge)(to_turn.wait_send)
    pl.when(jnp.logical_not(is_edge))(turned_to_ext.wait_send)
    pl.when(is_turn)(from_turn.wait_send)
    pl.when(is_end)(to_hub.wait_send)
    pl.when(jnp.logical_not(is_end))(rest_to_ext.wait_send)
    pl.when(is_spoke)(from_spoke.wait_send)

    @pl.when(is_hub)
    def _():
        to_spoke.wait_send()
        from_hub.wait_send()

    pl.loop(0, NCH - 1)(lambda c: block_to_ext(c).wait_send())
    pl.loop(0, NCH)(lambda c: block_to_sib(c).wait_send())

    @pl.loop(0, NCH - 1)
    def _(c):
        far_to_sib(rows_of(c), c).wait()
        far_to_ext(rows_of(c), c).wait()

    @pl.loop(0, 2)
    def _(c):
        far_to_sib(late_rows(c), NCH - 1 + c).wait()
        far_to_ext(late_rows(c), NCH - 1 + c).wait()


def on_device(coefficients, masks):
    n = lax.axis_size("pa")
    block = pltpu.VMEM((R, 2 * K), BF)
    norm = pltpu.VMEM((R, LW), BF)
    dma = pltpu.SemaphoreType.DMA
    return pl.pallas_call(
        functools.partial(kernel, n),
        out_shape=pltpu.VMEM((R, 5 * R), BF),
        in_specs=[pl.BlockSpec(memory_space=pltpu.HBM)] * 2,
        out_specs=pl.BlockSpec(memory_space=pltpu.VMEM),
        scratch_shapes=[
            block, block, block, norm, norm, norm, norm, norm, norm,
            pltpu.VMEM((G, R), BF), pltpu.VMEM((G, R), BF),
            pltpu.VMEM((R, R), BF), pltpu.VMEM((R, R), BF),
            pltpu.VMEM((LW, K), BF), pltpu.VMEM((K, LW), BF), pltpu.VMEM((G, LW), BF),
            pltpu.VMEM((G, R), jnp.int32),
            dma((NCH,)), dma,
            pltpu.VMEM((RR, 2 * K), BF),
            dma, dma, dma, dma, dma, dma, dma, dma((3,)),
            pltpu.SemaphoreType.REGULAR, pltpu.SemaphoreType.REGULAR,
            dma((NCH + 4,)), dma((NCH + 4,)), dma, dma,
            dma((NCH,)), dma((NCH,)), dma((2,)), dma((2,)),
            dma((NSEND,)), dma((NSEND,)), dma((NSEND,)), dma((NSEND,)),
        ],
        compiler_params=pltpu.CompilerParams(
            collective_id=0, has_side_effects=True, vmem_limit_bytes=56 * 1024 * 1024
        ),
        cost_estimate=pl.CostEstimate(
            flops=2 * 4 * R * R * 2 * K, bytes_accessed=4 * R * 2 * K, transcendentals=4 * R * R
        ),
        name="band",
    )(coefficients, masks.T)


def solution(mesh):
    return jax.shard_map(
        on_device, mesh=mesh, in_specs=(P("pa", None), P("pa", None)),
        out_specs=P("pa", None), check_vma=False,
    )
```

```python
import functools

import jax
import jax.numpy as jnp
from jax import lax
from jax.experimental import pallas as pl
from jax.experimental.pallas import tpu as pltpu
from jax.sharding import PartitionSpec as P

K = 1536
G = 48
R = 768
BF = jnp.bfloat16
F32 = jnp.float32
MESH = pl.DeviceIdType.MESH

ridge_term = 1.0

CH = 256
NCH = R // CH
LATE = CH // 2
NSEND = NCH + 1
LW = 256
ROWS = 768
KP = 256

NX = 4
NY = 4
RR = 48
TR = 32
TC = 2304
TE = 1920


def nt(x, y):
    return lax.dot_general(x, y, (((1,), (1,)), ((), ())), preferred_element_type=F32)


def nn(x, y):
    return jnp.dot(x, y, preferred_element_type=F32)


def tn(x, y):
    return lax.dot_general(x, y, (((0,), (0,)), ((), ())), preferred_element_type=F32)


def iota(shape, dim):
    return lax.broadcasted_iota(jnp.int32, shape, dim)


def lane_group(shape):
    lane = iota(shape, 1)
    lane = jnp.where(lane < G, lane, jnp.where(lane < 2 * G, lane - G, lane - 2 * G))
    return jnp.where(iota(shape, 1) < 3 * G, lane, K)


def remote(src, dst, send_sem, recv_sem, device):
    return pltpu.make_async_remote_copy(
        src_ref=src, dst_ref=dst, send_sem=send_sem, recv_sem=recv_sem,
        device_id=(device,), device_id_type=MESH,
    )


def rows_of(c):
    return pl.ds(pl.multiple_of(c * CH, CH), CH)


def late_rows(c):
    return pl.ds(pl.multiple_of(R - CH + c * LATE, LATE), LATE)


def kernel(n, coeff, masks, out, a, s, e, pa, ma, ps, ms, pe, me, mt, mte, far, fart,
           expand, group, rep, mask_in, load_sem, mask_sem,
           rb, turn_send, turn_recv, mid_send, mid_recv, mid_on_send, mid_on_recv,
           hub_send, hub_recv, spoke_send, spoke_recv,
           on_send, on_recv, leave, vouch, eb_send, eb_recv, em_send, em_recv, sb_send, sb_recv, sp_send, sp_recv,
           fe_send, fe_recv, fs_send, fs_recv):
    d = lax.axis_index("pa")
    odd = lax.rem(d, 2)
    sib = d + 1 - 2 * odd
    ext = lax.rem(d + n + 2 * odd - 1, n)
    band_s = (3 - 2 * odd) * R
    band_e = (1 + 2 * odd) * R
    band_far_e = 4 * odd * R
    band_far_s = (4 - 4 * odd) * R
    band_sib_far = 4 * odd * R
    band_ext_far = (4 - 4 * odd) * R

    row = 2 * NX
    plane = row * NY
    place = lax.rem(d, plane)
    base = d - place
    below = lax.rem(base + n - plane, n)
    above = lax.rem(base + plane, n)
    is_last = place == plane - 1
    is_first = place == 0
    is_end = is_last | is_first
    level = place // row
    is_up = (lax.rem(place, row) == row - 2) & (level < 2)
    is_down = (lax.rem(place, row) == 1) & (level >= NY - 2)
    column = lax.rem(place, row)
    is_edge = (column == 0) | (column == row - 1)
    is_turn_up = column == 3
    is_turn_down = column == row - 4
    is_turn = is_turn_up | is_turn_down
    turns_end = jnp.where(is_turn_up, level == 0, level == NY - 1)
    turns_mid = is_turn & jnp.logical_not(turns_end)
    is_mid = is_edge & jnp.logical_not(is_end)
    row_up = base + lax.rem(level + 1, NY) * row
    row_down = base + lax.rem(level + NY - 1, NY) * row
    turn_from = jnp.where(is_turn_up, row_down + row - 1, row_up)
    turn_to = lax.rem(turn_from + n + jnp.where(is_turn_up, 1, -1), n)

    def turn_of(edge):
        at = lax.rem(edge, plane)
        level = at // row
        up = lax.rem(level + 1, NY) * row + 3
        down = lax.rem(level + NY - 1, NY) * row + row - 4
        return edge - at + jnp.where(lax.rem(edge, 2) == 1, up, down)

    turn_out = turn_of(d)
    turn_in = turn_of(ext)
    level = jnp.where(is_up, level, NY - 1 - level)
    is_hub = (is_up | is_down) & (level == 0)
    is_spoke = (is_up | is_down) & (level == 1)
    step = jnp.where(is_up, row, -row)
    hub_from = base + jnp.where(is_up, plane - 1, 0)
    relay_to = jnp.where(is_up, above, below + plane - 1)
    hub_out = base + jnp.where(is_last, row - 2, plane - row + 1)
    hub_in = jnp.where(is_last, above + plane - row + 1, below + row - 2)
    spoke_in = hub_in + jnp.where(is_last, -row, row)

    def cols(band, rows):
        return pl.ds(pl.multiple_of(band + rows.start, rows.size), rows.size)

    def whole(band):
        return pl.ds(pl.multiple_of(band, R), R)

    load_mask = pltpu.make_async_copy(masks, mask_in, mask_sem)

    def load(c):
        return pltpu.make_async_copy(coeff.at[rows_of(c), :], a.at[rows_of(c), :], load_sem.at[c])

    def to_ext(rows, c):
        return remote(coeff.at[rows, :], e.at[rows, :], eb_send.at[c], eb_recv.at[c], ext)

    def block_to_ext(c):
        return to_ext(rows_of(c), c)

    late_to_ext = to_ext(late_rows(0), NCH - 1)
    turned = pl.ds(R - LATE, TR)
    turned_columns, mid_columns = pl.ds(0, TE), pl.ds(TE, TC - TE)
    kept_columns = pl.ds(TC, 2 * K - TC)

    def turned_rows_to_ext(columns, c):
        return remote(coeff.at[turned, columns], e.at[turned, columns],
                      eb_send.at[c], eb_recv.at[c], ext)

    turned_to_ext = turned_rows_to_ext(turned_columns, NCH + 2)
    kept_to_ext = turned_rows_to_ext(kept_columns, NCH + 3)
    most_to_ext = to_ext(pl.ds(R - LATE + TR, LATE - TR - RR), NCH)
    mid_to_ext = turned_rows_to_ext(mid_columns, NCH + 4)
    mid_at_turn = rb.at[0:TR, mid_columns]
    mid_to_turn = remote(coeff.at[turned, mid_columns], mid_at_turn, mid_send, mid_recv, turn_out)
    mid_from_turn = remote(mid_at_turn, e.at[turned, mid_columns], mid_on_send, mid_on_recv,
                           turn_to)
    at_turn = rb.at[0:TR, turned_columns]
    to_turn = remote(coeff.at[turned, turned_columns], at_turn, turn_send, turn_recv, turn_out)
    from_turn = remote(at_turn, e.at[turned, turned_columns], on_send, on_recv.at[2], turn_to)
    rest = pl.ds(R - RR, RR)
    rest_to_ext = to_ext(rest, NCH + 1)
    reals, imags = pl.ds(0, K), pl.ds(K, K)
    to_hub = remote(coeff.at[rest, :], rb, hub_send, hub_recv, hub_out)
    to_spoke = remote(rb.at[:, imags], rb.at[:, imags], spoke_send, spoke_recv, d + step)
    from_hub = remote(rb.at[:, reals], e.at[rest, reals], on_send, on_recv.at[0], relay_to)
    from_spoke = remote(rb.at[:, imags], e.at[rest, imags], on_send, on_recv.at[1], relay_to)

    def block_to_sib(c):
        return remote(a.at[rows_of(c), :], s.at[rows_of(c), :], sb_send.at[c], sb_recv.at[c], sib)

    def far_to_ext(rows, c):
        return remote(fart.at[rows, :], out.at[rows, whole(band_ext_far)],
                      fe_send.at[c], fe_recv.at[c], ext)

    def far_to_sib(rows, c):
        return remote(far.at[:, cols(0, rows)], out.at[:, cols(band_sib_far, rows)],
                      fs_send.at[c], fs_recv.at[c], sib)

    mask_to_ext = remote(mt, mte, em_send, em_recv, ext)
    m_to_sib = remote(ma, ms, sp_send.at[0], sp_recv.at[0], sib)
    p_to_sib = remote(pa, ps, sp_send.at[1], sp_recv.at[1], sib)

    barrier = pltpu.get_barrier_semaphore()
    pl.semaphore_signal(barrier, inc=1, device_id=(ext,), device_id_type=MESH)
    pl.semaphore_signal(barrier, inc=1, device_id=(sib,), device_id_type=MESH)

    def greet(device):
        pl.semaphore_signal(barrier, inc=1, device_id=(device,), device_id_type=MESH)

    @pl.when(is_hub)
    def _():
        greet(hub_from)

    @pl.when(is_hub | is_spoke)
    def _():
        greet(relay_to)

    @pl.when(is_turn)
    def _():
        greet(turn_to)

    load_mask.start()
    pl.loop(0, NCH)(lambda c: load(c).start())
    pl.semaphore_wait(barrier, jnp.where(is_end, 6, jnp.where(is_edge, 3, 2)))

    block_to_ext(0).start()

    def allow(device):
        pl.semaphore_signal(leave, inc=1, device_id=(device,), device_id_type=MESH)

    @pl.when(is_edge)
    def _():
        allow(turn_in)
        pl.semaphore_signal(vouch, inc=1, device_id=(ext,), device_id_type=MESH)

    @pl.when(is_end)
    def _():
        to_hub.start()
        allow(hub_in)
        allow(spoke_in)

    load_mask.wait()
    mt[...] = mask_in[...].astype(F32).astype(BF)
    mask_to_ext.start()
    pl.loop(1, NCH - 1)(lambda c: block_to_ext(c).start())
    late_to_ext.start()
    pl.when(jnp.logical_not(is_edge))(turned_to_ext.start)
    pl.when(jnp.logical_not(is_mid))(mid_to_ext.start)
    kept_to_ext.start()
    most_to_ext.start()
    pl.when(jnp.logical_not(is_end))(rest_to_ext.start)

    rep[...] = jnp.where(lane_group((G, LW)) == iota((G, LW), 0), 1.0, 0.0).astype(BF)
    ma[...] = tn(mt[...], rep[...]).astype(BF)
    m_to_sib.start()
    for k in range(0, K, KP):
        first = iota((LW, KP), 0) * (K // G)
        column = iota((LW, KP), 1) + k
        expand[:, k:k + KP] = jnp.where(
            (column >= first) & (column < first + K // G), 1.0, 0.0
        ).astype(BF)
        first = lane_group((KP, LW)) * (K // G)
        column = iota((KP, LW), 0) + k
        group[k:k + KP, :] = jnp.where(
            (column >= first) & (column < first + K // G), 1.0, 0.0
        ).astype(BF)

    def split(x):
        first = x.astype(BF)
        rest = x - first.astype(F32)
        second = rest.astype(BF)
        return first, second, (rest - second.astype(F32)).astype(BF)

    def prepare(rows, block, m, p):
        count = rows.size
        m_rows = m[rows, :]
        power = jnp.zeros((count, LW), F32)
        for k in range(0, K, KP):
            keep = nn(m_rows, expand[:, k:k + KP]).astype(BF)
            re = block[rows, k:k + KP] * keep
            im = block[rows, K + k:K + k + KP] * keep
            block[rows, k:k + KP] = re
            block[rows, K + k:K + k + KP] = im
            re = re.astype(F32)
            im = im.astype(F32)
            parts = nn(jnp.concatenate(split(re * re + im * im), axis=0), group[k:k + KP, :])
            power += parts[:count] + parts[count:2 * count] + parts[2 * count:]
        first, second, third = split(power)
        lane = iota((count, LW), 1)
        p[rows, :] = jnp.where(lane < G, first, jnp.where(lane < 2 * G, second, third))

    def score(x, px, mx, left, y, py, my, right):
        numerator = nt(x[left, :], y[right, :])
        norm_left = nt(px[left, :], my[right, :])
        norm_right = nt(mx[left, :], py[right, :])
        return numerator * lax.rsqrt((norm_left + ridge_term) * (norm_right + ridge_term))

    def near(rows, y, py, my, band):
        for i in range(0, R, ROWS):
            left = pl.ds(i, ROWS)
            out[left, cols(band, rows)] = score(a, pa, ma, left, y, py, my, rows).astype(BF)

    @pl.when(is_edge)
    def _():
        pl.semaphore_wait(vouch, 1)
        to_turn.start()
        pl.when(is_mid)(mid_to_turn.start)

    @pl.loop(0, NCH)
    def _(c):
        load(c).wait()
        prepare(rows_of(c), a, ma, pa)
        block_to_sib(c).start()

    p_to_sib.start()

    @pl.when(is_turn)
    def _():
        to_turn.wait_recv()
        pl.semaphore_wait(leave, 1)
        from_turn.start()

        @pl.when(turns_mid)
        def _():
            mid_to_turn.wait_recv()
            mid_from_turn.start()

    @pl.when(is_hub)
    def _():
        to_hub.wait_recv()
        pl.semaphore_wait(leave, 1)
        to_spoke.start()
        from_hub.start()

    @pl.loop(0, NCH)
    def _(c):
        near(rows_of(c), a, pa, ma, 2 * R)

    m_to_sib.wait_recv()
    p_to_sib.wait_recv()

    @pl.loop(0, NCH)
    def _(c):
        block_to_sib(c).wait_recv()
        near(rows_of(c), s, ps, ms, band_s)

    @pl.when(is_spoke)
    def _():
        to_spoke.wait_recv()
        pl.semaphore_wait(leave, 1)
        from_spoke.start()

    mask_to_ext.wait_recv()
    me[...] = tn(mte[...], rep[...]).astype(BF)

    def with_ext(rows, c):
        prepare(rows, e, me, pe)
        tile = score(e, pe, me, rows, s, ps, ms, pl.ds(0, R))
        fart[rows, :] = tile.astype(BF)

        @pl.when(c == NCH)
        def _():
            far_to_ext(rows, c).start()

        far[:, cols(0, rows)] = tile.T.astype(BF)
        far_to_sib(rows, c).start()
        near(rows, e, pe, me, band_e)

    @pl.loop(0, NCH - 1)
    def _(c):
        block_to_ext(c).wait_recv()
        pl.when(c > 0)(lambda: far_to_ext(rows_of(c - 1), c - 1).start())
        with_ext(rows_of(c), c)

    @pl.loop(0, 2)
    def _(c):
        @pl.when(c == 0)
        def _():
            late_to_ext.wait_recv()
            far_to_ext(rows_of(NCH - 2), NCH - 2).start()

        @pl.when(c == 1)
        def _():
            most_to_ext.wait_recv()
            kept_to_ext.wait_recv()
            pl.when(is_mid)(mid_from_turn.wait_recv)
            pl.when(jnp.logical_not(is_mid))(mid_to_ext.wait_recv)
            pl.when(is_edge)(from_turn.wait_recv)
            pl.when(jnp.logical_not(is_edge))(turned_to_ext.wait_recv)
            pl.when(jnp.logical_not(is_end))(rest_to_ext.wait_recv)

            @pl.when(is_end)
            def _():
                from_hub.wait_recv()
                from_spoke.wait_recv()

            far_to_ext(late_rows(0), NCH - 1).start()

        with_ext(late_rows(c), NCH - 1 + c)

    mask_to_ext.wait_send()
    m_to_sib.wait_send()
    p_to_sib.wait_send()
    late_to_ext.wait_send()
    most_to_ext.wait_send()
    kept_to_ext.wait_send()
    pl.when(is_mid)(mid_to_turn.wait_send)
    pl.when(jnp.logical_not(is_mid))(mid_to_ext.wait_send)
    pl.when(turns_mid)(mid_from_turn.wait_send)
    pl.when(is_edge)(to_turn.wait_send)
    pl.when(jnp.logical_not(is_edge))(turned_to_ext.wait_send)
    pl.when(is_turn)(from_turn.wait_send)
    pl.when(is_end)(to_hub.wait_send)
    pl.when(jnp.logical_not(is_end))(rest_to_ext.wait_send)
    pl.when(is_spoke)(from_spoke.wait_send)

    @pl.when(is_hub)
    def _():
        to_spoke.wait_send()
        from_hub.wait_send()

    pl.loop(0, NCH - 1)(lambda c: block_to_ext(c).wait_send())
    pl.loop(0, NCH)(lambda c: block_to_sib(c).wait_send())

    @pl.loop(0, NCH - 1)
    def _(c):
        far_to_sib(rows_of(c), c).wait()
        far_to_ext(rows_of(c), c).wait()

    @pl.loop(0, 2)
    def _(c):
        far_to_sib(late_rows(c), NCH - 1 + c).wait()
        far_to_ext(late_rows(c), NCH - 1 + c).wait()


def on_device(coefficients, masks):
    n = lax.axis_size("pa")
    block = pltpu.VMEM((R, 2 * K), BF)
    norm = pltpu.VMEM((R, LW), BF)
    dma = pltpu.SemaphoreType.DMA
    return pl.pallas_call(
        functools.partial(kernel, n),
        out_shape=pltpu.VMEM((R, 5 * R), BF),
        in_specs=[pl.BlockSpec(memory_space=pltpu.HBM)] * 2,
        out_specs=pl.BlockSpec(memory_space=pltpu.VMEM),
        scratch_shapes=[
            block, block, block, norm, norm, norm, norm, norm, norm,
            pltpu.VMEM((G, R), BF), pltpu.VMEM((G, R), BF),
            pltpu.VMEM((R, R), BF), pltpu.VMEM((R, R), BF),
            pltpu.VMEM((LW, K), BF), pltpu.VMEM((K, LW), BF), pltpu.VMEM((G, LW), BF),
            pltpu.VMEM((G, R), jnp.int32),
            dma((NCH,)), dma,
            pltpu.VMEM((RR, 2 * K), BF),
            dma, dma, dma, dma, dma, dma,
            dma, dma, dma, dma, dma, dma((3,)),
            pltpu.SemaphoreType.REGULAR, pltpu.SemaphoreType.REGULAR,
            dma((NCH + 5,)), dma((NCH + 5,)), dma, dma,
            dma((NCH,)), dma((NCH,)), dma((2,)), dma((2,)),
            dma((NSEND,)), dma((NSEND,)), dma((NSEND,)), dma((NSEND,)),
        ],
        compiler_params=pltpu.CompilerParams(
            collective_id=0, has_side_effects=True, vmem_limit_bytes=56 * 1024 * 1024
        ),
        cost_estimate=pl.CostEstimate(
            flops=2 * 4 * R * R * 2 * K, bytes_accessed=4 * R * 2 * K, transcendentals=4 * R * R
        ),
        name="band",
    )(coefficients, masks.T)


def solution(mesh):
    return jax.shard_map(
        on_device, mesh=mesh, in_specs=(P("pa", None), P("pa", None)),
        out_specs=P("pa", None), check_vma=False,
    )
```

```python
import functools

import jax
import jax.numpy as jnp
from jax import lax
from jax.experimental import pallas as pl
from jax.experimental.pallas import tpu as pltpu
from jax.sharding import PartitionSpec as P

K = 1536
G = 48
R = 768
BF = jnp.bfloat16
F32 = jnp.float32
MESH = pl.DeviceIdType.MESH

ridge_term = 1.0

CH = 256
NCH = R // CH
LATE = CH // 2
NSEND = NCH + 1
LW = 256
ROWS = 768
KP = 256

NX = 4
NY = 4
RR = 48
TR = 32
TC = 2304
TE = 1664


def nt(x, y):
    return lax.dot_general(x, y, (((1,), (1,)), ((), ())), preferred_element_type=F32)


def nn(x, y):
    return jnp.dot(x, y, preferred_element_type=F32)


def tn(x, y):
    return lax.dot_general(x, y, (((0,), (0,)), ((), ())), preferred_element_type=F32)


def iota(shape, dim):
    return lax.broadcasted_iota(jnp.int32, shape, dim)


def lane_group(shape):
    lane = iota(shape, 1)
    lane = jnp.where(lane < G, lane, jnp.where(lane < 2 * G, lane - G, lane - 2 * G))
    return jnp.where(iota(shape, 1) < 3 * G, lane, K)


def remote(src, dst, send_sem, recv_sem, device):
    return pltpu.make_async_remote_copy(
        src_ref=src, dst_ref=dst, send_sem=send_sem, recv_sem=recv_sem,
        device_id=(device,), device_id_type=MESH,
    )


def rows_of(c):
    return pl.ds(pl.multiple_of(c * CH, CH), CH)


def late_rows(c):
    return pl.ds(pl.multiple_of(R - CH + c * LATE, LATE), LATE)


def kernel(n, coeff, masks, out, a, s, e, pa, ma, ps, ms, pe, me, mt, mte, far, fart,
           expand, group, rep, mask_in, load_sem, mask_sem,
           rb, turn_send, turn_recv, mid_send, mid_recv, mid_on_send, mid_on_recv,
           hub_send, hub_recv, spoke_send, spoke_recv,
           on_send, on_recv, leave, vouch, eb_send, eb_recv, em_send, em_recv, sb_send, sb_recv, sp_send, sp_recv,
           fe_send, fe_recv, fs_send, fs_recv):
    d = lax.axis_index("pa")
    odd = lax.rem(d, 2)
    sib = d + 1 - 2 * odd
    ext = lax.rem(d + n + 2 * odd - 1, n)
    band_s = (3 - 2 * odd) * R
    band_e = (1 + 2 * odd) * R
    band_far_e = 4 * odd * R
    band_far_s = (4 - 4 * odd) * R
    band_sib_far = 4 * odd * R
    band_ext_far = (4 - 4 * odd) * R

    row = 2 * NX
    plane = row * NY
    place = lax.rem(d, plane)
    base = d - place
    below = lax.rem(base + n - plane, n)
    above = lax.rem(base + plane, n)
    is_last = place == plane - 1
    is_first = place == 0
    is_end = is_last | is_first
    level = place // row
    is_up = (lax.rem(place, row) == row - 2) & (level < 2)
    is_down = (lax.rem(place, row) == 1) & (level >= NY - 2)
    column = lax.rem(place, row)
    is_edge = (column == 0) | (column == row - 1)
    is_turn_up = column == 3
    is_turn_down = column == row - 4
    is_turn = is_turn_up | is_turn_down
    turns_end = jnp.where(is_turn_up, level == 0, level == NY - 1)
    turns_mid = is_turn & jnp.logical_not(turns_end)
    is_mid = is_edge & jnp.logical_not(is_end)
    row_up = base + lax.rem(level + 1, NY) * row
    row_down = base + lax.rem(level + NY - 1, NY) * row
    turn_from = jnp.where(is_turn_up, row_down + row - 1, row_up)
    turn_to = lax.rem(turn_from + n + jnp.where(is_turn_up, 1, -1), n)

    def turn_of(edge):
        at = lax.rem(edge, plane)
        level = at // row
        up = lax.rem(level + 1, NY) * row + 3
        down = lax.rem(level + NY - 1, NY) * row + row - 4
        return edge - at + jnp.where(lax.rem(edge, 2) == 1, up, down)

    turn_out = turn_of(d)
    turn_in = turn_of(ext)
    level = jnp.where(is_up, level, NY - 1 - level)
    is_hub = (is_up | is_down) & (level == 0)
    is_spoke = (is_up | is_down) & (level == 1)
    step = jnp.where(is_up, row, -row)
    hub_from = base + jnp.where(is_up, plane - 1, 0)
    relay_to = jnp.where(is_up, above, below + plane - 1)
    hub_out = base + jnp.where(is_last, row - 2, plane - row + 1)
    hub_in = jnp.where(is_last, above + plane - row + 1, below + row - 2)
    spoke_in = hub_in + jnp.where(is_last, -row, row)

    def cols(band, rows):
        return pl.ds(pl.multiple_of(band + rows.start, rows.size), rows.size)

    def whole(band):
        return pl.ds(pl.multiple_of(band, R), R)

    load_mask = pltpu.make_async_copy(masks, mask_in, mask_sem)

    def load(c):
        return pltpu.make_async_copy(coeff.at[rows_of(c), :], a.at[rows_of(c), :], load_sem.at[c])

    def to_ext(rows, c):
        return remote(coeff.at[rows, :], e.at[rows, :], eb_send.at[c], eb_recv.at[c], ext)

    def block_to_ext(c):
        return to_ext(rows_of(c), c)

    late_to_ext = to_ext(late_rows(0), NCH - 1)
    turned = pl.ds(R - LATE, TR)
    turned_columns, mid_columns = pl.ds(0, TE), pl.ds(TE, TC - TE)
    kept_columns = pl.ds(TC, 2 * K - TC)

    def turned_rows_to_ext(columns, c):
        return remote(coeff.at[turned, columns], e.at[turned, columns],
                      eb_send.at[c], eb_recv.at[c], ext)

    turned_to_ext = turned_rows_to_ext(turned_columns, NCH + 2)
    kept_to_ext = turned_rows_to_ext(kept_columns, NCH + 3)
    most_to_ext = to_ext(pl.ds(R - LATE + TR, LATE - TR - RR), NCH)
    mid_to_ext = turned_rows_to_ext(mid_columns, NCH + 4)
    mid_at_turn = rb.at[0:TR, mid_columns]
    mid_to_turn = remote(coeff.at[turned, mid_columns], mid_at_turn, mid_send, mid_recv, turn_out)
    mid_from_turn = remote(mid_at_turn, e.at[turned, mid_columns], mid_on_send, mid_on_recv,
                           turn_to)
    at_turn = rb.at[0:TR, turned_columns]
    to_turn = remote(coeff.at[turned, turned_columns], at_turn, turn_send, turn_recv, turn_out)
    from_turn = remote(at_turn, e.at[turned, turned_columns], on_send, on_recv.at[2], turn_to)
    rest = pl.ds(R - RR, RR)
    rest_to_ext = to_ext(rest, NCH + 1)
    reals, imags = pl.ds(0, K), pl.ds(K, K)
    to_hub = remote(coeff.at[rest, :], rb, hub_send, hub_recv, hub_out)
    to_spoke = remote(rb.at[:, imags], rb.at[:, imags], spoke_send, spoke_recv, d + step)
    from_hub = remote(rb.at[:, reals], e.at[rest, reals], on_send, on_recv.at[0], relay_to)
    from_spoke = remote(rb.at[:, imags], e.at[rest, imags], on_send, on_recv.at[1], relay_to)

    def block_to_sib(c):
        return remote(a.at[rows_of(c), :], s.at[rows_of(c), :], sb_send.at[c], sb_recv.at[c], sib)

    def far_to_ext(rows, c):
        return remote(fart.at[rows, :], out.at[rows, whole(band_ext_far)],
                      fe_send.at[c], fe_recv.at[c], ext)

    def far_to_sib(rows, c):
        return remote(far.at[:, cols(0, rows)], out.at[:, cols(band_sib_far, rows)],
                      fs_send.at[c], fs_recv.at[c], sib)

    mask_to_ext = remote(mt, mte, em_send, em_recv, ext)
    m_to_sib = remote(ma, ms, sp_send.at[0], sp_recv.at[0], sib)
    p_to_sib = remote(pa, ps, sp_send.at[1], sp_recv.at[1], sib)

    barrier = pltpu.get_barrier_semaphore()
    pl.semaphore_signal(barrier, inc=1, device_id=(ext,), device_id_type=MESH)
    pl.semaphore_signal(barrier, inc=1, device_id=(sib,), device_id_type=MESH)

    def greet(device):
        pl.semaphore_signal(barrier, inc=1, device_id=(device,), device_id_type=MESH)

    @pl.when(is_hub)
    def _():
        greet(hub_from)

    @pl.when(is_hub | is_spoke)
    def _():
        greet(relay_to)

    @pl.when(is_turn)
    def _():
        greet(turn_to)

    load_mask.start()
    pl.loop(0, NCH)(lambda c: load(c).start())
    pl.semaphore_wait(barrier, jnp.where(is_end, 6, jnp.where(is_edge, 3, 2)))

    block_to_ext(0).start()

    def allow(device):
        pl.semaphore_signal(leave, inc=1, device_id=(device,), device_id_type=MESH)

    @pl.when(is_edge)
    def _():
        allow(turn_in)
        pl.semaphore_signal(vouch, inc=1, device_id=(ext,), device_id_type=MESH)

    @pl.when(is_end)
    def _():
        to_hub.start()
        allow(hub_in)
        allow(spoke_in)

    load_mask.wait()
    mt[...] = mask_in[...].astype(F32).astype(BF)
    mask_to_ext.start()
    pl.loop(1, NCH - 1)(lambda c: block_to_ext(c).start())
    late_to_ext.start()
    pl.when(jnp.logical_not(is_edge))(turned_to_ext.start)
    pl.when(jnp.logical_not(is_mid))(mid_to_ext.start)
    kept_to_ext.start()
    most_to_ext.start()
    pl.when(jnp.logical_not(is_end))(rest_to_ext.start)

    rep[...] = jnp.where(lane_group((G, LW)) == iota((G, LW), 0), 1.0, 0.0).astype(BF)
    ma[...] = tn(mt[...], rep[...]).astype(BF)
    m_to_sib.start()
    for k in range(0, K, KP):
        first = iota((LW, KP), 0) * (K // G)
        column = iota((LW, KP), 1) + k
        expand[:, k:k + KP] = jnp.where(
            (column >= first) & (column < first + K // G), 1.0, 0.0
        ).astype(BF)
        first = lane_group((KP, LW)) * (K // G)
        column = iota((KP, LW), 0) + k
        group[k:k + KP, :] = jnp.where(
            (column >= first) & (column < first + K // G), 1.0, 0.0
        ).astype(BF)

    def split(x):
        first = x.astype(BF)
        rest = x - first.astype(F32)
        second = rest.astype(BF)
        return first, second, (rest - second.astype(F32)).astype(BF)

    def prepare(rows, block, m, p):
        count = rows.size
        m_rows = m[rows, :]
        power = jnp.zeros((count, LW), F32)
        for k in range(0, K, KP):
            keep = nn(m_rows, expand[:, k:k + KP]).astype(BF)
            re = block[rows, k:k + KP] * keep
            im = block[rows, K + k:K + k + KP] * keep
            block[rows, k:k + KP] = re
            block[rows, K + k:K + k + KP] = im
            re = re.astype(F32)
            im = im.astype(F32)
            parts = nn(jnp.concatenate(split(re * re + im * im), axis=0), group[k:k + KP, :])
            power += parts[:count] + parts[count:2 * count] + parts[2 * count:]
        first, second, third = split(power)
        lane = iota((count, LW), 1)
        p[rows, :] = jnp.where(lane < G, first, jnp.where(lane < 2 * G, second, third))

    def score(x, px, mx, left, y, py, my, right):
        numerator = nt(x[left, :], y[right, :])
        norm_left = nt(px[left, :], my[right, :])
        norm_right = nt(mx[left, :], py[right, :])
        return numerator * lax.rsqrt((norm_left + ridge_term) * (norm_right + ridge_term))

    def near(rows, y, py, my, band):
        for i in range(0, R, ROWS):
            left = pl.ds(i, ROWS)
            out[left, cols(band, rows)] = score(a, pa, ma, left, y, py, my, rows).astype(BF)

    @pl.when(is_edge)
    def _():
        pl.semaphore_wait(vouch, 1)
        to_turn.start()
        pl.when(is_mid)(mid_to_turn.start)

    @pl.loop(0, NCH)
    def _(c):
        load(c).wait()
        prepare(rows_of(c), a, ma, pa)
        block_to_sib(c).start()

    p_to_sib.start()

    @pl.when(is_turn)
    def _():
        to_turn.wait_recv()
        pl.semaphore_wait(leave, 1)
        from_turn.start()

        @pl.when(turns_mid)
        def _():
            mid_to_turn.wait_recv()
            mid_from_turn.start()

    @pl.when(is_hub)
    def _():
        to_hub.wait_recv()
        pl.semaphore_wait(leave, 1)
        to_spoke.start()
        from_hub.start()

    @pl.loop(0, NCH)
    def _(c):
        near(rows_of(c), a, pa, ma, 2 * R)

    m_to_sib.wait_recv()
    p_to_sib.wait_recv()

    @pl.loop(0, NCH)
    def _(c):
        block_to_sib(c).wait_recv()
        near(rows_of(c), s, ps, ms, band_s)

    @pl.when(is_spoke)
    def _():
        to_spoke.wait_recv()
        pl.semaphore_wait(leave, 1)
        from_spoke.start()

    mask_to_ext.wait_recv()
    me[...] = tn(mte[...], rep[...]).astype(BF)

    def with_ext(rows, c):
        prepare(rows, e, me, pe)
        tile = score(e, pe, me, rows, s, ps, ms, pl.ds(0, R))
        fart[rows, :] = tile.astype(BF)

        @pl.when(c == NCH)
        def _():
            far_to_ext(rows, c).start()

        far[:, cols(0, rows)] = tile.T.astype(BF)
        far_to_sib(rows, c).start()
        near(rows, e, pe, me, band_e)

    @pl.loop(0, NCH - 1)
    def _(c):
        block_to_ext(c).wait_recv()
        pl.when(c > 0)(lambda: far_to_ext(rows_of(c - 1), c - 1).start())
        with_ext(rows_of(c), c)

    @pl.loop(0, 2)
    def _(c):
        @pl.when(c == 0)
        def _():
            late_to_ext.wait_recv()
            far_to_ext(rows_of(NCH - 2), NCH - 2).start()

        @pl.when(c == 1)
        def _():
            most_to_ext.wait_recv()
            kept_to_ext.wait_recv()
            pl.when(is_mid)(mid_from_turn.wait_recv)
            pl.when(jnp.logical_not(is_mid))(mid_to_ext.wait_recv)
            pl.when(is_edge)(from_turn.wait_recv)
            pl.when(jnp.logical_not(is_edge))(turned_to_ext.wait_recv)
            pl.when(jnp.logical_not(is_end))(rest_to_ext.wait_recv)

            @pl.when(is_end)
            def _():
                from_hub.wait_recv()
                from_spoke.wait_recv()

            far_to_ext(late_rows(0), NCH - 1).start()

        with_ext(late_rows(c), NCH - 1 + c)

    mask_to_ext.wait_send()
    m_to_sib.wait_send()
    p_to_sib.wait_send()
    late_to_ext.wait_send()
    most_to_ext.wait_send()
    kept_to_ext.wait_send()
    pl.when(is_mid)(mid_to_turn.wait_send)
    pl.when(jnp.logical_not(is_mid))(mid_to_ext.wait_send)
    pl.when(turns_mid)(mid_from_turn.wait_send)
    pl.when(is_edge)(to_turn.wait_send)
    pl.when(jnp.logical_not(is_edge))(turned_to_ext.wait_send)
    pl.when(is_turn)(from_turn.wait_send)
    pl.when(is_end)(to_hub.wait_send)
    pl.when(jnp.logical_not(is_end))(rest_to_ext.wait_send)
    pl.when(is_spoke)(from_spoke.wait_send)

    @pl.when(is_hub)
    def _():
        to_spoke.wait_send()
        from_hub.wait_send()

    pl.loop(0, NCH - 1)(lambda c: block_to_ext(c).wait_send())
    pl.loop(0, NCH)(lambda c: block_to_sib(c).wait_send())

    @pl.loop(0, NCH - 1)
    def _(c):
        far_to_sib(rows_of(c), c).wait()
        far_to_ext(rows_of(c), c).wait()

    @pl.loop(0, 2)
    def _(c):
        far_to_sib(late_rows(c), NCH - 1 + c).wait()
        far_to_ext(late_rows(c), NCH - 1 + c).wait()


def on_device(coefficients, masks):
    n = lax.axis_size("pa")
    block = pltpu.VMEM((R, 2 * K), BF)
    norm = pltpu.VMEM((R, LW), BF)
    dma = pltpu.SemaphoreType.DMA
    return pl.pallas_call(
        functools.partial(kernel, n),
        out_shape=pltpu.VMEM((R, 5 * R), BF),
        in_specs=[pl.BlockSpec(memory_space=pltpu.HBM)] * 2,
        out_specs=pl.BlockSpec(memory_space=pltpu.VMEM),
        scratch_shapes=[
            block, block, block, norm, norm, norm, norm, norm, norm,
            pltpu.VMEM((G, R), BF), pltpu.VMEM((G, R), BF),
            pltpu.VMEM((R, R), BF), pltpu.VMEM((R, R), BF),
            pltpu.VMEM((LW, K), BF), pltpu.VMEM((K, LW), BF), pltpu.VMEM((G, LW), BF),
            pltpu.VMEM((G, R), jnp.int32),
            dma((NCH,)), dma,
            pltpu.VMEM((RR, 2 * K), BF),
            dma, dma, dma, dma, dma, dma,
            dma, dma, dma, dma, dma, dma((3,)),
            pltpu.SemaphoreType.REGULAR, pltpu.SemaphoreType.REGULAR,
            dma((NCH + 5,)), dma((NCH + 5,)), dma, dma,
            dma((NCH,)), dma((NCH,)), dma((2,)), dma((2,)),
            dma((NSEND,)), dma((NSEND,)), dma((NSEND,)), dma((NSEND,)),
        ],
        compiler_params=pltpu.CompilerParams(
            collective_id=0, has_side_effects=True, vmem_limit_bytes=56 * 1024 * 1024
        ),
        cost_estimate=pl.CostEstimate(
            flops=2 * 4 * R * R * 2 * K, bytes_accessed=4 * R * 2 * K, transcendentals=4 * R * R
        ),
        name="band",
    )(coefficients, masks.T)


def solution(mesh):
    return jax.shard_map(
        on_device, mesh=mesh, in_specs=(P("pa", None), P("pa", None)),
        out_specs=P("pa", None), check_vma=False,
    )
```
